256 devices in a mesh: dp: 32 (over x, y, core), expert: 8 (over z).
Axes of the slice: x: 4, y: 4, z: 8, core: 2. Of those that a mesh axis runs over, the one named last changes fastest.
Arguments:
- hidden: bfloat16 [12288, 2, 8192], P('dp', None, 'expert'), may hold values from -6 to 6
- out_grad: bfloat16 [12288, 3072], P('dp'), may hold values from -6 to 6
- gate_probs: float32 [12288, 2], P('dp'), may hold values from 0.1 to 1
- expert_ids: int32 [12288, 2], P('dp'), may hold values from 0 to 7, all different within a row; in each aligned block of 384 rows (0 to 383, 384 to 767, ...) at most 192 rows name the same one
- base_down: bfloat16 [8192, 3072], P('expert', 'dp'), may hold values from -0.0625 to 0.0625
- delta_in: bfloat16 [8, 8192, 256], P(None, 'expert'), may hold values from -0.0625 to 0.0625
- delta_out: bfloat16 [8, 256, 3072], P('expert'), may hold values from -0.375 to 0.375
Outputs:
- grad_hidden: bfloat16 [12288, 2, 8192], P('dp', None, 'expert')
- grad_gate: float32 [12288, 2], P('dp')
- grad_base: float32 [8192, 3072], P('expert', 'dp')
- grad_delta_in: float32 [8, 8192, 256], P(None, 'expert', 'dp')
- grad_delta_out: float32 [8, 256, 3072], P('expert', None, 'dp')
The draws below stay inside these ranges and needn't reach their ends.
Inputs may be any that keep to these rules, and one draw needn't show every extreme that they name: `expert_ids`: the two experts of a token differ. In every token group of 384 tokens no expert is named by more than 192 slots, and in some group some expert is named by exactly 192 slots.
All inputs are finite; a program needn't handle non-finite values.
Results may differ from the reference program's by a relative error of at most 0.027.
Values may be sent and summed in bfloat16 or wider, within the bound.
No kernel may reach another device: no remote copies, remote signals or barrier semaphores. Data moves between devices by JAX's collectives and lax.ppermute only.
A program may use at most 128 MiB of HBM per device.

```python
import math
import jax
import jax.numpy as jnp
import numpy as np
from jax import lax

D = 3072
FF = 8192
R = 256
TOP = 2
TOK_G = 384
E = 8
CAP = 192
TOKENS = 12288
N_DP = 32
N_EXPERT = 8


def spiked(values, own_key, source, target, shards_of, factor):
    owner, partner = [(jnp.arange(values.shape[dim]) // (values.shape[dim] // shards_of)).reshape([-1 if axis == dim else 1 for axis in range(values.ndim)]) for dim in (source, target)]
    chosen = jax.random.permutation(own_key, shards_of)[partner]
    strong = (owner == chosen) | (owner == (partner + shards_of // 2) % shards_of)
    return jnp.where(strong, factor * values, values)


def block_scale(own_key, shape, shards, smallest, largest):
    level, own = 1.0, jax.random.fold_in(own_key, 6)
    for axis_at, blocks in shards:
        draws = jnp.exp(jax.random.uniform(jax.random.fold_in(own, axis_at), (blocks,), jnp.float32, smallest / len(shards), largest / len(shards)))
        level = level * jnp.repeat(draws, shape[axis_at] // blocks).reshape([-1 if axis == axis_at else 1 for axis in range(len(shape))])
    return level


def deal_out(stream_key, own, number, rows, number_of, top, limit, lean):
    ranking = jax.random.permutation(stream_key, number_of)
    crowded, usual = load_shares(number_of, rows * top, limit, lean, True), load_shares(number_of, rows * top, limit, lean, False)
    places = jnp.arange(number_of)

    def named(tallies, offset_by):
        used = int((tallies > 0).sum())
        fixed = max(1, used // 4)
        shifted = fixed + (places - fixed + offset_by * (used - fixed)) % max(1, number_of - fixed)
        return jnp.zeros((number_of,), jnp.int32).at[ranking[jnp.where(places < fixed, places, shifted)]].set(jnp.asarray(tallies, jnp.int32))

    tallies = jnp.where(number % 4 == 0, named(crowded, number // 4), named(usual, number - number // 4 - 1))
    mixed = jax.random.permutation(jax.random.fold_in(own, 3), number_of)
    giver, receiver = mixed[0:number_of // 2 * 2:2], mixed[1:number_of // 2 * 2:2]
    slack = jnp.minimum(tallies[giver] - 1, limit - tallies[receiver]) // 2
    slack = jnp.where((giver == ranking[0]) | (receiver == ranking[0]) | (tallies[receiver] == 0), 0, jnp.maximum(slack, 0))
    shifted = jax.random.randint(jax.random.fold_in(own, 4), (number_of // 2,), 0, 1 << 20) % (slack + 1)
    tallies = tallies.at[giver].add(-shifted).at[receiver].add(shifted)
    labels = jnp.searchsorted(jnp.cumsum(tallies), jnp.arange(rows * top), side="right").astype(jnp.int32)
    table = labels.reshape(top, rows).T
    table = table[jax.random.permutation(jax.random.fold_in(own, 1), rows)]
    offset_by = jax.random.randint(jax.random.fold_in(own, 2), (rows, 1), 0, top)
    return jnp.take_along_axis(table, (jnp.arange(top)[None, :] + offset_by) % top, axis=1)


def load_shares(number_of, total, bound, lean, full):
    weights = [(1 << 20) // math.isqrt(grade ** lean) + 1 for grade in range(1, number_of + 1)]
    largest = bound if full else min(bound, max(-(-total // number_of), total * weights[0] // sum(weights)))
    least = 1 if total - largest >= number_of - 1 else 0
    counts, rest = [largest] + [least] * (number_of - 1), total - largest - least * (number_of - 1)
    while rest > 0:
        movable = [i for i in range(1, number_of) if counts[i] < largest] or [i for i in range(1, number_of) if counts[i] < bound]
        mass, budget = sum([weights[i] for i in movable]), rest
        for i in movable:
            more = min(bound - counts[i], max(1, budget * weights[i] // mass), rest)
            counts[i] = counts[i] + more
            rest = rest - more
    return np.array(counts)


def noise(rng, dims, spread, bound, shards=(), kind=jnp.bfloat16):
    values = jax.random.normal(rng, dims, jnp.float32) * spread
    if len(shards) > 0:
        values = block_scale(rng, dims, shards, -0.22, 0.18) * values
    return jnp.clip(values, min=-bound, max=bound).astype(kind)


def noise_with(stream_key, shape, spread, limit, shards, heavy, kind=jnp.bfloat16):
    array = spread * jax.random.normal(stream_key, shape, jnp.float32)
    if shards:
        array = array * block_scale(stream_key, shape, shards, -0.22, 0.18)
    return jnp.clip(spiked(array, jax.random.fold_in(stream_key, 3), *heavy), -limit, limit).astype(kind)


def setup_inputs(seed: int = 0) -> dict:
    splits = jax.random.split(jax.random.key(seed), 8)
    hidden = noise(splits[0], (TOKENS, TOP, FF), 1.0, 6.0, ((0, 32), (2, 8)))
    out_grad = noise_with(splits[1], (TOKENS, D), 1.0, 6.0, ((0, 32),), (0, 1, 32, 2.75))
    gate_probs = jnp.clip(jnp.exp(math.log(1.0) - 2.3025851 * jax.random.uniform(splits[2], (TOKENS, TOP), jnp.float32) ** block_scale(splits[2], (TOKENS, TOP), ((0, 32),), -0.2, 0.2)), 0.1, 1.0)
    expert_ids_keys = jax.random.split(jax.random.fold_in(splits[3], 1), TOKENS // TOK_G)
    expert_ids_turns = jax.random.permutation(jax.random.fold_in(splits[3], 3), TOKENS // TOK_G)
    expert_ids = jax.vmap(lambda own, number: deal_out(jax.random.fold_in(splits[3], 2), own, number, TOK_G, N_EXPERT, 2, CAP, 1))(expert_ids_keys, expert_ids_turns).reshape((TOKENS, TOP))
    base_down = noise(splits[4], (FF, D), FF ** -0.5, 0.0625, ((0, 8), (1, 32)))
    delta_in = noise(splits[5], (E, FF, R), FF ** -0.5, 0.0625, ((1, 8),))
    delta_out = noise(splits[6], (E, R, D), R ** -0.5, 0.375, ((0, 8),))
    return {"hidden": hidden, "out_grad": out_grad, "gate_probs": gate_probs, "expert_ids": expert_ids, "base_down": base_down, "delta_in": delta_in, "delta_out": delta_out}


def reference(hidden, out_grad, gate_probs, expert_ids, base_down, delta_in, delta_out):
    in_wide = delta_in.astype(jnp.float32)
    out_wide = delta_out.astype(jnp.float32)
    slots = TOK_G * TOP

    def group_pass(carry, pieces):
        base_acc, in_acc, out_acc = carry
        hid, grad, gate, ids = pieces
        ids_flat = ids.reshape(slots).astype(jnp.int32)
        onehot = (ids_flat[:, None] == jnp.arange(E, dtype=jnp.int32)[None, :]).astype(jnp.int32)
        within = jnp.sum((jnp.cumsum(onehot, axis=0) - onehot) * onehot, axis=1).astype(jnp.int32)
        dest = (ids_flat * CAP + within).astype(jnp.int32)
        source = jnp.zeros((E * CAP,), jnp.int32).at[dest].set(jnp.arange(slots, dtype=jnp.int32))
        filled = jnp.zeros((E * CAP,), jnp.int32).at[dest].set(1) > 0
        hid_flat = hid.reshape(slots, FF)
        proj = jnp.dot(grad, base_down.T, preferred_element_type=jnp.float32)
        scaled = (gate[:, :, None] * grad[:, None, :].astype(jnp.float32)).astype(jnp.bfloat16).reshape(slots, D)
        base_part = jnp.dot(hid_flat.T, scaled, preferred_element_type=jnp.float32)
        hid_pad = jnp.where(filled[:, None], hid_flat[source], 0).reshape(E, CAP, FF)
        latent = jnp.einsum("ecf,efr->ecr", hid_pad.astype(jnp.float32), in_wide)
        token_pad = (source // TOP).astype(jnp.int32)
        grad_pad = jnp.where(filled[:, None], grad[token_pad], 0).reshape(E, CAP, D)
        coef = jnp.einsum("ecd,erd->ecr", grad_pad.astype(jnp.float32), out_wide).astype(jnp.bfloat16)
        gate_pad = jnp.where(filled, gate.reshape(slots)[source], 0.0).reshape(E, CAP)
        weighted = (gate_pad[:, :, None] * coef.astype(jnp.float32)).astype(jnp.bfloat16)
        scaled_pad = jnp.where(filled[:, None], scaled[source], 0).reshape(E, CAP, D)
        latent_b = lax.optimization_barrier(latent.astype(jnp.bfloat16))
        out_part = jnp.einsum("ecr,ecd->erd", latent_b.astype(jnp.float32), scaled_pad.astype(jnp.float32))
        in_part = jnp.einsum("ecf,ecr->efr", hid_pad.astype(jnp.float32), weighted.astype(jnp.float32))
        back_pad = jnp.einsum("ecr,efr->ecf", coef.astype(jnp.float32), in_wide).reshape(E * CAP, FF)
        back = proj[:, None, :] + back_pad[dest].reshape(TOK_G, TOP, FF)
        grad_hidden = (gate[:, :, None] * back).astype(jnp.bfloat16)
        grad_gate = jnp.sum(hid.astype(jnp.float32) * back, axis=-1)
        in_round = lax.optimization_barrier(in_part.astype(jnp.bfloat16))
        out_round = lax.optimization_barrier(out_part.astype(jnp.bfloat16))
        carry = (base_acc + base_part, in_acc + in_round.astype(jnp.float32), out_acc + out_round.astype(jnp.float32))
        return carry, (grad_hidden, grad_gate)

    start = (jnp.zeros((FF, D), jnp.float32), jnp.zeros((E, FF, R), jnp.float32), jnp.zeros((E, R, D), jnp.float32))
    pieces = (hidden.reshape(N_DP, TOK_G, TOP, FF), out_grad.reshape(N_DP, TOK_G, D),
              gate_probs.reshape(N_DP, TOK_G, TOP), expert_ids.reshape(N_DP, TOK_G, TOP))
    sums, per_group = lax.scan(group_pass, start, pieces)
    grad_hidden = per_group[0].reshape(TOKENS, TOP, FF)
    grad_gate = per_group[1].reshape(TOKENS, TOP)
    return grad_hidden, grad_gate, sums[0], sums[1], sums[2]
```

```python
import functools

import jax
import jax.numpy as jnp
import numpy as np
from jax import lax
from jax.experimental import pallas as pl
from jax.experimental.pallas import tpu as pltpu
from jax.sharding import PartitionSpec as P

BF = jnp.bfloat16
F32 = jnp.float32
NX = NY = 4
NZ = 8
NDP = 32
CAP = 192
VMEM = 50 * 1024 * 1024
CHEAP = pl.CostEstimate(flops=1000, bytes_accessed=1000, transcendentals=0)

SIDE_A = (1, 0, 3, 2)
SIDE_B = (3, 2, 1, 0)
GRAY = (0, 1, 3, 2)
LINKS = (
    (("yb", "ya", "xb", "xa"), ("yb", "ya", "xa", "xb")),
    (("xb", "xa", "yb", "ya"), ("xb", "xa", "ya", "yb")),
)


def dp_index(x, y, c):
    return (x * NY + y) * 2 + c


def neighbour(x, y, link):
    side = SIDE_A if link[1] == "a" else SIDE_B
    return (side[x], y) if link[0] == "x" else (x, side[y])


def step_pairs(stream, *bits):
    pairs = []
    for x in range(NX):
        for y in range(NY):
            for c in range(2):
                nx, ny = x, y
                for t in bits:
                    nx, ny = neighbour(nx, ny, LINKS[c][stream][t])
                pairs.append((dp_index(x, y, c), dp_index(nx, ny, c)))
    return pairs


CORE_PAIRS = [(i, i ^ 1) for i in range(NDP)]


def position_table():
    table = np.zeros((NDP, 2, NDP), np.int32)
    for x in range(NX):
        for y in range(NY):
            for c in range(2):
                for s in range(2):
                    for u in range(NX):
                        for v in range(NY):
                            for d in range(2):
                                differ = {
                                    "xa": (GRAY[x] ^ GRAY[u]) & 1,
                                    "xb": (GRAY[x] ^ GRAY[u]) >> 1,
                                    "ya": (GRAY[y] ^ GRAY[v]) & 1,
                                    "yb": (GRAY[y] ^ GRAY[v]) >> 1,
                                }
                                place = 16 * (c ^ d)
                                for t in range(4):
                                    place += differ[LINKS[d][s][t]] << t
                                table[dp_index(x, y, c), s, dp_index(u, v, d)] = place
    rows = 32 * (table // 16) + table % 16 + 16 * np.arange(2).reshape(1, 2, 1)
    return np.concatenate([rows.reshape(NDP, 2 * NDP), table.reshape(NDP, 2 * NDP)], axis=1).astype(np.int32)


def z_table():
    table = np.zeros((NZ, NZ), np.int32)
    for z in range(NZ):
        held = [z, z ^ 1]
        back, ahead = (z - 2) % NZ, (z + 2) % NZ
        far = (z + 4) % NZ
        held += [back, back ^ 1, ahead, ahead ^ 1, far, far ^ 1]
        for place, e in enumerate(held):
            table[z, e] = place
    return table


def params(**kw):
    return pltpu.CompilerParams(vmem_limit_bytes=VMEM, **kw)


def mm(a, b):
    return jnp.dot(a, b, preferred_element_type=F32)


def mm_nt(a, b):
    return lax.dot_general(a, b, (((1,), (1,)), ((), ())), preferred_element_type=F32)


def front_kernel(pos, own, ids_ref, gate_ref, og_ref, dout_ref, rows_ref, cols_ref, coef_ref, ogt_ref, acc):
    j = pl.program_id(0)
    tok = og_ref.shape[0]

    @pl.when(j == 0)
    def _():
        ids0, ids1 = ids_ref[0:1, :], ids_ref[1:2, :]
        g0, g1 = gate_ref[0:1, :], gate_ref[1:2, :]
        e = lax.broadcasted_iota(jnp.int32, (NZ, tok), 0)
        m0 = (e == ids0).astype(F32)
        m1 = (e == ids1).astype(F32)
        both = m0 + m1
        before = lax.broadcasted_iota(jnp.int32, (tok, tok), 0) < lax.broadcasted_iota(
            jnp.int32, (tok, tok), 1
        )
        rank = mm(both.astype(BF), before.astype(F32).astype(BF))
        rank = jnp.where(both > 0, rank, -1.0)
        rows_ref[...] = rank
        gates = m0 * g0 + m1 * g1
        ends = jnp.concatenate([g0, g1, jnp.zeros((6, tok), F32)], axis=0)
        wide = jnp.concatenate(
            [rank, m0, m1, gates, ends, jnp.zeros((88, tok), F32)], axis=0
        )
        cols_ref[...] = wide.T
        acc[...] = jnp.zeros_like(acc)

    og = og_ref[...]
    acc[...] += mm_nt(og, dout_ref[0])
    turned = og.T
    for b in range(4):
        for s in range(2):
            at = b * 96 + s * 48
            ogt_ref[pos[s * NDP + 4 * j + b]] = turned[at : at + 48]

    @pl.when(j == pl.num_programs(0) - 1)
    def _():
        rank = rows_ref[pl.ds(own[0], 1), :]
        slot = lax.broadcasted_iota(jnp.int32, (CAP, tok), 0).astype(F32)
        pick = (slot == rank).astype(F32).astype(BF)
        coef_ref[...] = mm(pick, acc[...].astype(BF)).astype(BF)


def front(pos, own, ids, gate, og, dout):
    tok, width = og.shape
    rank = dout.shape[1]
    chunk = 384
    return pl.pallas_call(
        front_kernel,
        out_shape=(
            jax.ShapeDtypeStruct((NZ, tok), F32),
            jax.ShapeDtypeStruct((tok, 128), F32),
            jax.ShapeDtypeStruct((CAP, rank), BF),
            jax.ShapeDtypeStruct((2 * NDP, 48, tok), BF),
        ),
        grid_spec=pltpu.PrefetchScalarGridSpec(
            num_scalar_prefetch=2,
            grid=(width // chunk,),
            in_specs=[
                pl.BlockSpec((2, tok), lambda j, p, o: (0, 0)),
                pl.BlockSpec((2, tok), lambda j, p, o: (0, 0)),
                pl.BlockSpec((tok, chunk), lambda j, p, o: (0, j)),
                pl.BlockSpec((1, rank, chunk), lambda j, p, o: (0, 0, j)),
            ],
            out_specs=[
                pl.BlockSpec((NZ, tok), lambda j, p, o: (0, 0)),
                pl.BlockSpec((tok, 128), lambda j, p, o: (0, 0)),
                pl.BlockSpec((CAP, rank), lambda j, p, o: (0, 0)),
                pl.BlockSpec((2 * NDP, 48, tok), lambda j, p, o: (0, 0, 0)),
            ],
            scratch_shapes=[pltpu.VMEM((tok, rank), F32)],
        ),
        compiler_params=params(),
        cost_estimate=CHEAP,
        name="front",
    )(pos, own, ids, gate, og, dout)


def chosen(h_ref, second):
    second = jnp.broadcast_to(second, h_ref.shape[1:]).astype(BF)
    return h_ref[0] * (1 - second) + h_ref[1] * second


def latent_kernel(after, rows_ref, cols_ref, h_ref, din_ref, out_ref):
    i = pl.program_id(0)
    tok = h_ref.shape[1]
    lane = lax.broadcasted_iota(jnp.int32, cols_ref.shape, 1)
    slot = lax.broadcasted_iota(jnp.int32, (CAP, tok), 0).astype(F32)
    for n in range(2):
        e = 2 * i + n
        second = jnp.sum(jnp.where(lane == 16 + e, cols_ref[...], 0.0), axis=1, keepdims=True)
        lat = mm(chosen(h_ref, second), din_ref[n]).astype(BF)
        pick = (slot == rows_ref[pl.ds(e, 1), :]).astype(F32).astype(BF)
        out_ref[n] = mm(pick, lat).astype(BF)


def latents(after, rows, cols, hk, din):
    tok, ff = hk.shape[1:]
    rank = din.shape[2]
    return pl.pallas_call(
        latent_kernel,
        out_shape=jax.ShapeDtypeStruct((NZ, CAP, rank), BF),
        grid_spec=pltpu.PrefetchScalarGridSpec(
            num_scalar_prefetch=1,
            grid=(NZ // 2,),
            in_specs=[
                pl.BlockSpec((NZ, tok), lambda e, a: (0, 0)),
                pl.BlockSpec((tok, 128), lambda e, a: (0, 0)),
                pl.BlockSpec((2, tok, ff), lambda e, a: (0, 0, 0)),
                pl.BlockSpec((2, ff, rank), lambda e, a: (e, 0, 0)),
            ],
            out_specs=pl.BlockSpec((2, CAP, rank), lambda e, a: (e, 0, 0)),
        ),
        compiler_params=params(),
        cost_estimate=CHEAP,
        name="latents",
    )(after, rows, cols, hk, din)


def base_kernel(after, cols_ref, h_ref, ogt_ref, send_ref, keep_ref, hg):
    i = pl.program_id(0)

    @pl.when(i == 0)
    def _():
        g0, g1 = column(cols_ref[...], 32), column(cols_ref[...], 33)
        hg[...] = (g0 * h_ref[0].astype(F32) + g1 * h_ref[1].astype(F32)).astype(BF)

    out = mm(ogt_ref[...], hg[...]).astype(BF)

    @pl.when(i < pl.num_programs(0) // 2)
    def _():
        send_ref[...] = out

    @pl.when(i >= pl.num_programs(0) // 2)
    def _():
        keep_ref[...] = out


def base_part(after, cols, hk, ogt):
    tok, ff = hk.shape[1:]
    rows = ogt.shape[0]
    tile, steps = rows // 8, 8
    half = jax.ShapeDtypeStruct((rows // 2, ff), BF)
    return pl.pallas_call(
        base_kernel,
        out_shape=(half, half),
        grid_spec=pltpu.PrefetchScalarGridSpec(
            num_scalar_prefetch=1,
            grid=(steps,),
            in_specs=[
                pl.BlockSpec((tok, 128), lambda i, a: (0, 0)),
                pl.BlockSpec((2, tok, ff), lambda i, a: (0, 0, 0)),
                pl.BlockSpec((tile, tok), lambda i, a: ((i + 4) % 8, 0)),
            ],
            out_specs=[
                pl.BlockSpec((tile, ff), lambda i, a: (jnp.minimum(i, 3), 0)),
                pl.BlockSpec((tile, ff), lambda i, a: (jnp.maximum(i - 4, 0), 0)),
            ],
            scratch_shapes=[pltpu.VMEM((tok, ff), BF)],
        ),
        compiler_params=params(),
        cost_estimate=CHEAP,
        name="base_part",
    )(after, cols, hk, ogt)


def column(cols, at):
    return cols[:, at : at + 1]


def delta_in_kernel(pos, zpos, cols_ref, ca_ref, cb_ref, h_ref, keep_ref, send_ref, ct_ref, turned):
    i = pl.program_id(0)
    s = i // 2
    tok = h_ref.shape[1]
    lane = lax.broadcasted_iota(jnp.int32, cols_ref.shape, 1)
    slot = lax.broadcasted_iota(jnp.int32, (tok, CAP), 1).astype(F32)
    parts = []
    for n, c_ref in enumerate((ca_ref, cb_ref)):
        e = 2 * i + n

        def col(base):
            return jnp.sum(jnp.where(lane == base + e, cols_ref[...], 0.0), axis=1, keepdims=True)

        spread = (slot == col(0)).astype(F32).astype(BF)
        coef = mm(spread, c_ref[0])
        ct_ref[n] = coef.astype(BF)
        weighted = (col(24) * coef).T
        for d in range(NDP):
            turned[pos[(2 + s) * NDP + d]] = weighted[8 * d : 8 * d + 8]
        w = turned[...].reshape(NDP * 8, tok).astype(BF)
        hid = chosen(h_ref, col(16))
        parts.append(mm(w, hid).reshape(NDP, 8, h_ref.shape[2]))
    both = jnp.concatenate(parts, axis=1).astype(BF)
    keep_ref[0, :, 0] = both[:16]
    send_ref[0, :, 0] = both[16:]


def delta_in_part(pos, zpos, cols, coefs, hk):
    tok, ff = hk.shape[1:]
    rank = coefs.shape[2]
    half = jax.ShapeDtypeStruct((2, 16, 2, 16, ff), BF)
    half_spec = pl.BlockSpec((1, 16, 1, 16, ff), lambda i, p, z: (i // 2, 0, i % 2, 0, 0))
    return pl.pallas_call(
        delta_in_kernel,
        out_shape=(half, half, jax.ShapeDtypeStruct((NZ, tok, rank), BF)),
        grid_spec=pltpu.PrefetchScalarGridSpec(
            num_scalar_prefetch=2,
            grid=(NZ // 2,),
            in_specs=[
                pl.BlockSpec((tok, 128), lambda i, p, z: (0, 0)),
                pl.BlockSpec((1, CAP, rank), lambda i, p, z: (z[2 * i], 0, 0)),
                pl.BlockSpec((1, CAP, rank), lambda i, p, z: (z[2 * i + 1], 0, 0)),
                pl.BlockSpec((2, tok, ff), lambda i, p, z: (0, 0, 0)),
            ],
            out_specs=[
                half_spec,
                half_spec,
                pl.BlockSpec((2, tok, rank), lambda i, p, z: (i, 0, 0)),
            ],
            scratch_shapes=[pltpu.VMEM((NDP, 8, tok), F32)],
        ),
        compiler_params=params(),
        cost_estimate=CHEAP,
        name="delta_in_part",
    )(pos, zpos, cols, coefs, coefs, hk)


def delta_out_kernel(own, cols_ref, lat_ref, ogt_ref, out_ref, spread):
    tok = cols_ref.shape[0]

    @pl.when(pl.program_id(0) == 0)
    def _():
        lane = lax.broadcasted_iota(jnp.int32, cols_ref.shape, 1)
        cols = cols_ref[...]
        rank = jnp.sum(jnp.where(lane == own[0], cols, 0.0), axis=1, keepdims=True)
        gate = jnp.sum(jnp.where(lane == 24 + own[0], cols, 0.0), axis=1, keepdims=True)
        slot = lax.broadcasted_iota(jnp.int32, (tok, CAP), 1).astype(F32)
        pick = (slot == rank).astype(F32).astype(BF)
        spread[...] = (gate * mm(pick, lat_ref[...])).astype(BF)

    out_ref[...] = mm(ogt_ref[...], spread[...]).astype(BF)


def delta_out_part(own, cols, lat, ogt):
    rows, tok = ogt.shape
    rank = lat.shape[1]
    tile = rows // 4
    return pl.pallas_call(
        delta_out_kernel,
        out_shape=jax.ShapeDtypeStruct((rows, rank), BF),
        grid_spec=pltpu.PrefetchScalarGridSpec(
            num_scalar_prefetch=1,
            grid=(4,),
            in_specs=[
                pl.BlockSpec((tok, 128), lambda i, o: (0, 0)),
                pl.BlockSpec((CAP, rank), lambda i, o: (0, 0)),
                pl.BlockSpec((tile, tok), lambda i, o: (i, 0)),
            ],
            out_specs=pl.BlockSpec((tile, rank), lambda i, o: (i, 0)),
            scratch_shapes=[pltpu.VMEM((tok, rank), BF)],
        ),
        compiler_params=params(),
        cost_estimate=CHEAP,
        name="delta_out_part",
    )(own, cols, lat, ogt)


def back_kernel(after, cols_ref, ogt_ref, w_own, w_other, ct_ref, din_ref, h_ref, gh_ref, gg_ref, og, lhs):
    n = pl.program_id(0)
    cols = cols_ref[...]
    quarter = ogt_ref.shape[0] // 4
    rank = ct_ref.shape[2]

    @pl.when(n == 0)
    def _():
        for a in range(4):
            og[:, a * quarter : (a + 1) * quarter] = ogt_ref[a * quarter : (a + 1) * quarter, :].T
        for e in range(NZ):
            coef = ct_ref[e].astype(F32)
            for k in range(2):
                lhs[k, :, e * rank : (e + 1) * rank] = (column(cols, 8 + 8 * k + e) * coef).astype(BF)
        gg_ref[...] = jnp.zeros_like(gg_ref)

    proj = mm(og[:, : 2 * quarter], w_own[...]) + mm(og[:, 2 * quarter :], w_other[...])
    for k in range(2):
        delta = mm_nt(lhs[k, :, :rank], din_ref[0])
        for e in range(1, NZ):
            delta = delta + mm_nt(lhs[k, :, e * rank : (e + 1) * rank], din_ref[e])
        back = proj + delta
        gh_ref[k] = (column(cols, 32 + k) * back).astype(BF)
        gg_ref[k] += jnp.sum(h_ref[k].astype(F32) * back, axis=1, keepdims=True)


def back_pass(after, cols, ogt, w_own, w_other, ct, din, hk):
    tok, ff = hk.shape[1:]
    rows = ogt.shape[0]
    rank = din.shape[2]
    tile = 256
    w_spec = pl.BlockSpec((rows // 2, tile), lambda n, a: (0, n))
    return pl.pallas_call(
        back_kernel,
        out_shape=(
            jax.ShapeDtypeStruct((2, tok, ff), BF),
            jax.ShapeDtypeStruct((2, tok, 1), F32),
        ),
        grid_spec=pltpu.PrefetchScalarGridSpec(
            num_scalar_prefetch=1,
            grid=(ff // tile,),
            in_specs=[
                pl.BlockSpec((tok, 128), lambda n, a: (0, 0)),
                pl.BlockSpec((rows, tok), lambda n, a: (0, 0)),
                w_spec,
                w_spec,
                pl.BlockSpec((NZ, tok, rank), lambda n, a: (0, 0, 0)),
                pl.BlockSpec((NZ, tile, rank), lambda n, a: (0, n, 0)),
                pl.BlockSpec((2, tok, tile), lambda n, a: (0, 0, n)),
            ],
            out_specs=[
                pl.BlockSpec((2, tok, tile), lambda n, a: (0, 0, n)),
                pl.BlockSpec((2, tok, 1), lambda n, a: (0, 0, 0)),
            ],
            scratch_shapes=[pltpu.VMEM((tok, rows), BF), pltpu.VMEM((2, tok, NZ * rank), BF)],
        ),
        compiler_params=params(),
        cost_estimate=CHEAP,
        name="back_pass",
    )(after, cols, ogt, w_own, w_other, ct, din, hk)


def add(a, b):
    return (a.astype(F32) + b.astype(F32)).astype(BF)


def tie_kernel(*refs):
    del refs


def tie(arrays):
    return pl.pallas_call(
        tie_kernel,
        out_shape=tuple(jax.ShapeDtypeStruct(v.shape, v.dtype) for v in arrays),
        in_specs=[pl.BlockSpec(memory_space=pl.ANY)] * len(arrays),
        out_specs=tuple(pl.BlockSpec(memory_space=pl.ANY) for _ in arrays),
        input_output_aliases={i: i for i in range(len(arrays))},
        compiler_params=pltpu.CompilerParams(has_side_effects=False, vmem_limit_bytes=1024 * 1024),
        cost_estimate=CHEAP,
        name="tie",
    )(*arrays)


def exchange(sends, pins):
    arrays = [v for v, _, _ in sends] + list(pins)
    arrays = tie(arrays)
    got = [lax.ppermute(v, axis, pairs) for v, (_, axis, pairs) in zip(arrays, sends)]
    return got, arrays[len(sends) :]


def core(v):
    return (v, "dp", CORE_PAIRS)


def wide(sends, t):
    return [(sends[s], "dp", step_pairs(s, t)) for s in range(2)]


LOW = ((0,), (1,), (0, 1))


def low(blocks):
    return [(v, "dp", step_pairs(0, *bits)) for v, bits in zip(blocks, LOW)]


def split(keep, got, n):
    stay = [add(k[:n], g[:n]) for k, g in zip(keep, got)]
    go = [add(k[n : 2 * n], g[n : 2 * n]) for k, g in zip(keep, got)]
    return stay, go


def split_low(keep, got):
    out = [
        jnp.stack([add(k[i : i + 1], g[i : i + 1]) for k, g in zip(keep, got)]) for i in range(4)
    ]
    return out[0], out[1:]


def last(keep, got):
    total = keep.astype(F32)
    for g in got:
        total = total + g.astype(F32)
    return total


def by_z(v, by):
    return (v, "expert", [(z, (z + by) % NZ) for z in range(NZ)])


def across_z(v, by):
    return (v, "expert", [(z, z ^ by) for z in range(NZ)])


def on_device(hidden, out_grad, gate_probs, expert_ids, base_down, delta_in, delta_out):
    tok, _, ff = hidden.shape
    width = out_grad.shape[1]
    rank = delta_in.shape[2]
    dp, own = lax.axis_index("dp"), lax.axis_index("expert")
    pos = lax.dynamic_index_in_dim(jnp.asarray(position_table()), dp, 0, keepdims=False)
    zpos = lax.dynamic_index_in_dim(jnp.asarray(z_table()), own, 0, keepdims=False)
    own = own.astype(jnp.int32).reshape(1)

    block = base_down.T.reshape(2, 1, 48, ff)
    got, (pos,) = exchange(low([block] * 3), [pos])
    held = [jnp.concatenate([block[s]] + [g[s] for g in got], axis=0) for s in range(2)]
    rows, cols, coef_mine, ogt = front(pos, own, expert_ids.T, gate_probs.T, out_grad, delta_out)
    ogt = ogt.reshape(width, tok)
    hk = jnp.transpose(hidden, (1, 0, 2))

    got, (own1, coef_mine) = exchange(
        wide(held, 2) + [across_z(coef_mine, 1)], [own, coef_mine]
    )
    held = [jnp.concatenate([held[s], got[s]], axis=0) for s in range(2)]
    pair = jnp.stack([coef_mine, got[2]])
    lat = latents(own1, rows, cols, hk, delta_in)

    got, (own2, lat) = exchange(wide(held, 3) + [by_z(pair, 2), by_z(pair, -2)], [own1, lat])
    w_own = jnp.stack([jnp.concatenate([held[s], got[s]], axis=0) for s in range(2)])
    back, ahead = got[2:]
    latent_b = lax.psum_scatter(lat, "expert", scatter_dimension=0, tiled=True)[0]
    send, keep = base_part(own2, cols, hk, ogt)

    base_keep = keep.reshape(2, 16, 48, ff)
    got, (own3,) = exchange(
        [core(w_own), core(send.reshape(2, 16, 48, ff)), by_z(back[:1], 2), by_z(ahead[1:], -2)],
        [own2],
    )
    w_other = got[0]
    coefs = jnp.concatenate([pair, back, ahead, got[2], got[3]], axis=0)
    base_keep, base_go = split(base_keep, got[1], 8)

    got, (zpos, own4) = exchange(wide(base_go, 3), [zpos, own3])
    in_keep, in_send, ct = delta_in_part(pos, zpos, cols, coefs, hk)
    base_keep, base_go = split(base_keep, got, 4)
    in_keep = in_keep.reshape(2, 16, 32, ff)

    got, (own5,) = exchange(wide(base_go, 2) + [core(in_send.reshape(2, 16, 32, ff))], [own4])
    gh, gg = back_pass(
        own5, cols, ogt, w_own.reshape(width // 2, ff), w_other.reshape(width // 2, ff), ct, delta_in, hk
    )
    base_keep, base_go = split_low(base_keep, got)
    in_keep, in_go = split(in_keep, got[2], 8)

    got, (gg, own6) = exchange(low(base_go) + wide(in_go, 3), [gg.reshape(2, tok), own5])
    grad_hidden = jnp.transpose(gh, (1, 0, 2))
    grad_base = last(base_keep, got[:3]).reshape(96, ff).T
    in_keep, in_go = split(in_keep, got[3:], 4)
    out_part = delta_out_part(own6, cols, latent_b, ogt).reshape(2, 2, 16, 48, rank)

    got, _ = exchange(wide(in_go, 2) + [core(out_part[1]), across_z(gg, 1)], [])
    in_keep, in_go = split_low(in_keep, got)
    gg = gg + got[3]
    cut = [
        [add(out_part[0, r, 4 * i : 4 * i + 4], got[2][r, 4 * i : 4 * i + 4]) for r in range(2)]
        for i in range(4)
    ]
    out_keep = jnp.stack(cut[0])
    out_go = [
        jnp.stack([cut[1][0], cut[2][1]]),
        jnp.stack([cut[2][0], cut[1][1]]),
        jnp.stack(cut[3]),
    ]

    got, _ = exchange(
        low(in_go)
        + [(v, "dp", step_pairs(0, *bits)) for v, bits in zip(out_go, ((2,), (3,), (2, 3)))]
        + [across_z(gg, 2)],
        [],
    )
    grad_delta_in = jnp.transpose(last(in_keep, got[:3]).reshape(NZ, 8, ff), (0, 2, 1))
    gg = gg + got[6]
    total = last(out_keep, got[3:6]).astype(BF)

    got, _ = exchange(low([total[:, i : i + 1] for i in (1, 2, 3)]) + [across_z(gg, 4)], [])
    grad_delta_out = last(total[:, :1], got[:3]).reshape(96, rank).T[None]
    gg = gg + got[3]
    return grad_hidden, gg.T, grad_base, grad_delta_in, grad_delta_out


def solution(mesh):
    in_specs = (
        P("dp", None, "expert"),
        P("dp", None),
        P("dp", None),
        P("dp", None),
        P("expert", "dp"),
        P(None, "expert", None),
        P("expert", None, None),
    )
    out_specs = (
        P("dp", None, "expert"),
        P("dp", None),
        P("expert", "dp"),
        P(None, "expert", "dp"),
        P("expert", None, "dp"),
    )
    return jax.shard_map(
        on_device, mesh=mesh, in_specs=in_specs, out_specs=out_specs, check_vma=False
    )
```

```python
import jax
import jax.numpy as jnp
import numpy as np
from jax import lax
from jax.experimental import pallas as pl
from jax.experimental.pallas import tpu as pltpu
from jax.sharding import PartitionSpec as P

BF = jnp.bfloat16
F32 = jnp.float32
NX = NY = 4
NZ = 8
NDP = 32
CAP = 192
VMEM = 50 * 1024 * 1024
CHEAP = pl.CostEstimate(flops=1000, bytes_accessed=1000, transcendentals=0)

SIDE_A = (1, 0, 3, 2)
SIDE_B = (3, 2, 1, 0)
GRAY = (0, 1, 3, 2)
LINKS = (
    (("yb", "ya", "xb", "xa"), ("yb", "ya", "xa", "xb")),
    (("xb", "xa", "yb", "ya"), ("xb", "xa", "ya", "yb")),
)


def dp_index(x, y, c):
    return (x * NY + y) * 2 + c


def neighbour(x, y, link):
    side = SIDE_A if link[1] == "a" else SIDE_B
    return (side[x], y) if link[0] == "x" else (x, side[y])


def step_pairs(stream, *bits):
    pairs = []
    for x in range(NX):
        for y in range(NY):
            for c in range(2):
                nx, ny = x, y
                for t in bits:
                    nx, ny = neighbour(nx, ny, LINKS[c][stream][t])
                pairs.append((dp_index(x, y, c), dp_index(nx, ny, c)))
    return pairs


CORE_PAIRS = [(i, i ^ 1) for i in range(NDP)]


def position_table():
    table = np.zeros((NDP, 2, NDP), np.int32)
    for x in range(NX):
        for y in range(NY):
            for c in range(2):
                for s in range(2):
                    for u in range(NX):
                        for v in range(NY):
                            for d in range(2):
                                differ = {
                                    "xa": (GRAY[x] ^ GRAY[u]) & 1,
                                    "xb": (GRAY[x] ^ GRAY[u]) >> 1,
                                    "ya": (GRAY[y] ^ GRAY[v]) & 1,
                                    "yb": (GRAY[y] ^ GRAY[v]) >> 1,
                                }
                                place = 16 * (c ^ d)
                                for t in range(4):
                                    place += differ[LINKS[d][s][t]] << t
                                table[dp_index(x, y, c), s, dp_index(u, v, d)] = place
    rows = 32 * (table // 16) + table % 16 + 16 * np.arange(2).reshape(1, 2, 1)
    return np.concatenate([rows.reshape(NDP, 2 * NDP), table.reshape(NDP, 2 * NDP)], axis=1).astype(np.int32)


def z_table():
    table = np.zeros((NZ, NZ), np.int32)
    for z in range(NZ):
        held = [z, z ^ 1]
        back, ahead = (z - 2) % NZ, (z + 2) % NZ
        far = (z + 4) % NZ
        held += [back, back ^ 1, ahead, ahead ^ 1, far, far ^ 1]
        for place, e in enumerate(held):
            table[z, e] = place
    return table


def params(**kw):
    return pltpu.CompilerParams(vmem_limit_bytes=VMEM, **kw)


def mm(a, b):
    return jnp.dot(a, b, preferred_element_type=F32)


def mm_nt(a, b):
    return lax.dot_general(a, b, (((1,), (1,)), ((), ())), preferred_element_type=F32)


def front_kernel(pos, own, ids_ref, gate_ref, og_ref, dout_ref, rows_ref, cols_ref, coef_ref, ogt_ref, acc):
    j = pl.program_id(0)
    tok = og_ref.shape[0]

    @pl.when(j == 0)
    def _():
        ids0, ids1 = ids_ref[0:1, :], ids_ref[1:2, :]
        g0, g1 = gate_ref[0:1, :], gate_ref[1:2, :]
        e = lax.broadcasted_iota(jnp.int32, (NZ, tok), 0)
        m0 = (e == ids0).astype(F32)
        m1 = (e == ids1).astype(F32)
        both = m0 + m1
        before = lax.broadcasted_iota(jnp.int32, (tok, tok), 0) < lax.broadcasted_iota(
            jnp.int32, (tok, tok), 1
        )
        rank = mm(both.astype(BF), before.astype(F32).astype(BF))
        rank = jnp.where(both > 0, rank, -1.0)
        rows_ref[...] = rank
        gates = m0 * g0 + m1 * g1
        ends = jnp.concatenate([g0, g1, jnp.zeros((6, tok), F32)], axis=0)
        wide = jnp.concatenate(
            [rank, m0, m1, gates, ends, jnp.zeros((88, tok), F32)], axis=0
        )
        cols_ref[...] = wide.T
        acc[...] = jnp.zeros_like(acc)

    og = og_ref[...]
    acc[...] += mm_nt(og, dout_ref[0])
    turned = og.T
    for b in range(4):
        for s in range(2):
            at = b * 96 + s * 48
            ogt_ref[pos[s * NDP + 4 * j + b]] = turned[at : at + 48]

    @pl.when(j == pl.num_programs(0) - 1)
    def _():
        rank = rows_ref[pl.ds(own[0], 1), :]
        slot = lax.broadcasted_iota(jnp.int32, (CAP, tok), 0).astype(F32)
        pick = (slot == rank).astype(F32).astype(BF)
        coef_ref[...] = mm(pick, acc[...].astype(BF)).astype(BF)


def front(pos, own, ids, gate, og, dout):
    tok, width = og.shape
    rank = dout.shape[1]
    chunk = 384
    return pl.pallas_call(
        front_kernel,
        out_shape=(
            jax.ShapeDtypeStruct((NZ, tok), F32),
            jax.ShapeDtypeStruct((tok, 128), F32),
            jax.ShapeDtypeStruct((CAP, rank), BF),
            jax.ShapeDtypeStruct((2 * NDP, 48, tok), BF),
        ),
        grid_spec=pltpu.PrefetchScalarGridSpec(
            num_scalar_prefetch=2,
            grid=(width // chunk,),
            in_specs=[
                pl.BlockSpec((2, tok), lambda j, p, o: (0, 0)),
                pl.BlockSpec((2, tok), lambda j, p, o: (0, 0)),
                pl.BlockSpec((tok, chunk), lambda j, p, o: (0, j)),
                pl.BlockSpec((1, rank, chunk), lambda j, p, o: (0, 0, j)),
            ],
            out_specs=[
                pl.BlockSpec((NZ, tok), lambda j, p, o: (0, 0)),
                pl.BlockSpec((tok, 128), lambda j, p, o: (0, 0)),
                pl.BlockSpec((CAP, rank), lambda j, p, o: (0, 0)),
                pl.BlockSpec((2 * NDP, 48, tok), lambda j, p, o: (0, 0, 0)),
            ],
            scratch_shapes=[pltpu.VMEM((tok, rank), F32)],
        ),
        compiler_params=params(),
        cost_estimate=CHEAP,
        name="front",
    )(pos, own, ids, gate, og, dout)


def chosen(h_ref, second):
    second = jnp.broadcast_to(second, h_ref.shape[1:]).astype(BF)
    return h_ref[0] * (1 - second) + h_ref[1] * second


def latent_kernel(after, rows_ref, cols_ref, h_ref, din_ref, out_ref):
    i = pl.program_id(0)
    tok = h_ref.shape[1]
    lane = lax.broadcasted_iota(jnp.int32, cols_ref.shape, 1)
    slot = lax.broadcasted_iota(jnp.int32, (CAP, tok), 0).astype(F32)
    for n in range(2):
        e = 2 * i + n
        second = jnp.sum(jnp.where(lane == 16 + e, cols_ref[...], 0.0), axis=1, keepdims=True)
        lat = mm(chosen(h_ref, second), din_ref[n]).astype(BF)
        pick = (slot == rows_ref[pl.ds(e, 1), :]).astype(F32).astype(BF)
        out_ref[n] = mm(pick, lat).astype(BF)


def latents(after, rows, cols, hk, din):
    tok, ff = hk.shape[1:]
    rank = din.shape[2]
    return pl.pallas_call(
        latent_kernel,
        out_shape=jax.ShapeDtypeStruct((NZ, CAP, rank), BF),
        grid_spec=pltpu.PrefetchScalarGridSpec(
            num_scalar_prefetch=1,
            grid=(NZ // 2,),
            in_specs=[
                pl.BlockSpec((NZ, tok), lambda e, a: (0, 0)),
                pl.BlockSpec((tok, 128), lambda e, a: (0, 0)),
                pl.BlockSpec((2, tok, ff), lambda e, a: (0, 0, 0)),
                pl.BlockSpec((2, ff, rank), lambda e, a: (e, 0, 0)),
            ],
            out_specs=pl.BlockSpec((2, CAP, rank), lambda e, a: (e, 0, 0)),
        ),
        compiler_params=params(),
        cost_estimate=CHEAP,
        name="latents",
    )(after, rows, cols, hk, din)


def base_kernel(after, hg_ref, ogt_ref, out_ref):
    out_ref[...] = mm(ogt_ref[...], hg_ref[...]).astype(BF)


def base_part(after, hg, ogt, half):
    tok, ff = hg.shape
    rows = ogt.shape[0] // 2
    tile, steps = rows // 4, 4
    return pl.pallas_call(
        base_kernel,
        out_shape=jax.ShapeDtypeStruct((rows, ff), BF),
        grid_spec=pltpu.PrefetchScalarGridSpec(
            num_scalar_prefetch=1,
            grid=(steps,),
            in_specs=[
                pl.BlockSpec((tok, ff), lambda i, a: (0, 0)),
                pl.BlockSpec((tile, tok), lambda i, a: (i + steps * half, 0)),
            ],
            out_specs=pl.BlockSpec((tile, ff), lambda i, a: (i, 0)),
        ),
        compiler_params=params(),
        cost_estimate=CHEAP,
        name="base_part",
    )(after, hg, ogt)


def merge_kernel(*refs):
    count = len(refs) - 2
    for s in range(2):
        at = 0
        for p in range(count // 2):
            piece = refs[2 * p + s]
            n = piece.shape[0]
            refs[count + s][at : at + n] = piece[...]
            at += n


def merge(pieces):
    flat = [v for pair in pieces for v in pair]
    n = sum(pair[0].shape[0] for pair in pieces)
    out = jax.ShapeDtypeStruct((n,) + flat[0].shape[1:], BF)
    return pl.pallas_call(
        merge_kernel,
        out_shape=(out, out),
        compiler_params=params(),
        cost_estimate=CHEAP,
        name="merge",
    )(*flat)


def merge_low_kernel(a_ref, b_ref, c_ref, d_ref, first_ref, second_ref):
    for p, piece in enumerate((a_ref, b_ref, c_ref, d_ref)):
        first_ref[p] = piece[0, 0]
        second_ref[p] = piece[1, 0]


def merge_low(pieces):
    out = jax.ShapeDtypeStruct((4,) + pieces[0].shape[2:], BF)
    return pl.pallas_call(
        merge_low_kernel,
        out_shape=(out, out),
        compiler_params=params(),
        cost_estimate=CHEAP,
        name="merge_low",
    )(*pieces)


def merge_all_kernel(a0, a1, b0, b1, out_ref):
    for s, (a, b) in enumerate(((a0, b0), (a1, b1))):
        n = a.shape[0]
        out_ref[s, :n] = a[...]
        out_ref[s, n:] = b[...]


def merge_all(a, b):
    n = a[0].shape[0]
    return pl.pallas_call(
        merge_all_kernel,
        out_shape=jax.ShapeDtypeStruct((2, 2 * n) + a[0].shape[1:], BF),
        compiler_params=params(),
        cost_estimate=CHEAP,
        name="merge_all",
    )(*a, *b)


def column(cols, at):
    return cols[:, at : at + 1]


def delta_in_kernel(pos, zpos, cols_ref, ca_ref, cb_ref, h_ref, keep_ref, send_ref, ct_ref, turned):
    i = pl.program_id(0)
    s = i // 2
    tok = h_ref.shape[1]
    lane = lax.broadcasted_iota(jnp.int32, cols_ref.shape, 1)
    slot = lax.broadcasted_iota(jnp.int32, (tok, CAP), 1).astype(F32)
    parts = []
    for n, c_ref in enumerate((ca_ref, cb_ref)):
        e = 2 * i + n

        def col(base):
            return jnp.sum(jnp.where(lane == base + e, cols_ref[...], 0.0), axis=1, keepdims=True)

        spread = (slot == col(0)).astype(F32).astype(BF)
        coef = mm(spread, c_ref[0])
        ct_ref[n] = coef.astype(BF)
        weighted = (col(24) * coef).T
        for d in range(NDP):
            turned[pos[(2 + s) * NDP + d]] = weighted[8 * d : 8 * d + 8]
        w = turned[...].reshape(NDP * 8, tok).astype(BF)
        hid = chosen(h_ref, col(16))
        parts.append(mm(w, hid).reshape(NDP, 8, h_ref.shape[2]))
    both = jnp.concatenate(parts, axis=1).astype(BF)
    keep_ref[0, :, 0] = both[:16]
    send_ref[0, :, 0] = both[16:]


def delta_in_part(pos, zpos, cols, coefs, hk):
    tok, ff = hk.shape[1:]
    rank = coefs.shape[2]
    half = jax.ShapeDtypeStruct((2, 16, 2, 16, ff), BF)
    half_spec = pl.BlockSpec((1, 16, 1, 16, ff), lambda i, p, z: (i // 2, 0, i % 2, 0, 0))
    return pl.pallas_call(
        delta_in_kernel,
        out_shape=(half, half, jax.ShapeDtypeStruct((NZ, tok, rank), BF)),
        grid_spec=pltpu.PrefetchScalarGridSpec(
            num_scalar_prefetch=2,
            grid=(NZ // 2,),
            in_specs=[
                pl.BlockSpec((tok, 128), lambda i, p, z: (0, 0)),
                pl.BlockSpec((1, CAP, rank), lambda i, p, z: (z[2 * i], 0, 0)),
                pl.BlockSpec((1, CAP, rank), lambda i, p, z: (z[2 * i + 1], 0, 0)),
                pl.BlockSpec((2, tok, ff), lambda i, p, z: (0, 0, 0)),
            ],
            out_specs=[
                half_spec,
                half_spec,
                pl.BlockSpec((2, tok, rank), lambda i, p, z: (i, 0, 0)),
            ],
            scratch_shapes=[pltpu.VMEM((NDP, 8, tok), F32)],
        ),
        compiler_params=params(),
        cost_estimate=CHEAP,
        name="delta_in_part",
    )(pos, zpos, cols, coefs, coefs, hk)


def delta_out_kernel(own, cols_ref, lat_ref, keep_rows, send_rows, keep_ref, send_ref, spread):
    tok = cols_ref.shape[0]

    @pl.when(pl.program_id(0) == 0)
    def _():
        lane = lax.broadcasted_iota(jnp.int32, cols_ref.shape, 1)
        cols = cols_ref[...]
        rank = jnp.sum(jnp.where(lane == own[0], cols, 0.0), axis=1, keepdims=True)
        gate = jnp.sum(jnp.where(lane == 24 + own[0], cols, 0.0), axis=1, keepdims=True)
        slot = lax.broadcasted_iota(jnp.int32, (tok, CAP), 1).astype(F32)
        pick = (slot == rank).astype(F32).astype(BF)
        spread[...] = (gate * mm(pick, lat_ref[...])).astype(BF)

    keep_ref[...] = mm(keep_rows[...], spread[...]).astype(BF)
    send_ref[...] = mm(send_rows[...], spread[...]).astype(BF)


def delta_out_part(own, cols, lat, ogt):
    rows, tok = ogt.shape
    rank = lat.shape[1]
    tile = rows // 4
    half = jax.ShapeDtypeStruct((rows // 2, rank), BF)
    return pl.pallas_call(
        delta_out_kernel,
        out_shape=(half, half),
        grid_spec=pltpu.PrefetchScalarGridSpec(
            num_scalar_prefetch=1,
            grid=(2,),
            in_specs=[
                pl.BlockSpec((tok, 128), lambda i, o: (0, 0)),
                pl.BlockSpec((CAP, rank), lambda i, o: (0, 0)),
                pl.BlockSpec((tile, tok), lambda i, o: (i, 0)),
                pl.BlockSpec((tile, tok), lambda i, o: (i + 2, 0)),
            ],
            out_specs=[pl.BlockSpec((tile, rank), lambda i, o: (i, 0))] * 2,
            scratch_shapes=[pltpu.VMEM((tok, rank), BF)],
        ),
        compiler_params=params(),
        cost_estimate=CHEAP,
        name="delta_out_part",
    )(own, cols, lat, ogt, ogt)


def back_kernel(after, cols_ref, ogt_ref, w_own, w_other, ct_ref, din_ref, h_ref, gh_ref, gg_ref, og, lhs):
    n = pl.program_id(0)
    cols = cols_ref[...]
    quarter = ogt_ref.shape[0] // 4
    rank = ct_ref.shape[2]

    @pl.when(n == 0)
    def _():
        for a in range(4):
            og[:, a * quarter : (a + 1) * quarter] = ogt_ref[a * quarter : (a + 1) * quarter, :].T
        for e in range(NZ):
            coef = ct_ref[e].astype(F32)
            for k in range(2):
                lhs[k, :, e * rank : (e + 1) * rank] = (column(cols, 8 + 8 * k + e) * coef).astype(BF)
        gg_ref[...] = jnp.zeros_like(gg_ref)

    proj = mm(og[:, : 2 * quarter], w_own[...]) + mm(og[:, 2 * quarter :], w_other[...])
    for k in range(2):
        delta = mm_nt(lhs[k, :, :rank], din_ref[0])
        for e in range(1, NZ):
            delta = delta + mm_nt(lhs[k, :, e * rank : (e + 1) * rank], din_ref[e])
        back = proj + delta
        gh_ref[k] = (column(cols, 32 + k) * back).astype(BF)
        gg_ref[k] += jnp.sum(h_ref[k].astype(F32) * back, axis=1, keepdims=True)


def back_pass(after, cols, ogt, w_own, w_other, ct, din, hk):
    tok, ff = hk.shape[1:]
    rows = ogt.shape[0]
    rank = din.shape[2]
    tile = 256
    w_spec = pl.BlockSpec((rows // 2, tile), lambda n, a: (0, n))
    return pl.pallas_call(
        back_kernel,
        out_shape=(
            jax.ShapeDtypeStruct((2, tok, ff), BF),
            jax.ShapeDtypeStruct((2, tok, 1), F32),
        ),
        grid_spec=pltpu.PrefetchScalarGridSpec(
            num_scalar_prefetch=1,
            grid=(ff // tile,),
            in_specs=[
                pl.BlockSpec((tok, 128), lambda n, a: (0, 0)),
                pl.BlockSpec((rows, tok), lambda n, a: (0, 0)),
                w_spec,
                w_spec,
                pl.BlockSpec((NZ, tok, rank), lambda n, a: (0, 0, 0)),
                pl.BlockSpec((NZ, tile, rank), lambda n, a: (0, n, 0)),
                pl.BlockSpec((2, tok, tile), lambda n, a: (0, 0, n)),
            ],
            out_specs=[
                pl.BlockSpec((2, tok, tile), lambda n, a: (0, 0, n)),
                pl.BlockSpec((2, tok, 1), lambda n, a: (0, 0, 0)),
            ],
            scratch_shapes=[pltpu.VMEM((tok, rows), BF), pltpu.VMEM((2, tok, NZ * rank), BF)],
        ),
        compiler_params=params(),
        cost_estimate=CHEAP,
        name="back_pass",
    )(after, cols, ogt, w_own, w_other, ct, din, hk)


def add(a, b):
    return (a.astype(F32) + b.astype(F32)).astype(BF)


def tie_kernel(*refs):
    del refs


def tie(arrays):
    return pl.pallas_call(
        tie_kernel,
        out_shape=tuple(jax.ShapeDtypeStruct(v.shape, v.dtype) for v in arrays),
        in_specs=[pl.BlockSpec(memory_space=pl.ANY)] * len(arrays),
        out_specs=tuple(pl.BlockSpec(memory_space=pl.ANY) for _ in arrays),
        input_output_aliases={i: i for i in range(len(arrays))},
        compiler_params=pltpu.CompilerParams(has_side_effects=False, vmem_limit_bytes=1024 * 1024),
        cost_estimate=CHEAP,
        name="tie",
    )(*arrays)


def exchange(sends, pins):
    arrays, places = [], []
    for v in [v for v, _, _ in sends] + list(pins):
        same = [i for i, w in enumerate(arrays) if w is v]
        places.append(same[0] if same else len(arrays))
        if not same:
            arrays.append(v)
    tied = tie(arrays)
    tied = [tied[i] for i in places]
    got = [lax.ppermute(v, axis, pairs) for v, (_, axis, pairs) in zip(tied, sends)]
    return got, tied[len(sends) :], tied[: len(sends)]


def core(v):
    return (v, "dp", CORE_PAIRS)


def wide(sends, t):
    return [(sends[s], "dp", step_pairs(s, t)) for s in range(2)]


LOW = ((0,), (1,), (0, 1))


def low(blocks):
    return [(v, "dp", step_pairs(0, *bits)) for v, bits in zip(blocks, LOW)]


def split(keep, got, n):
    stay = [add(k[:n], g[:n]) for k, g in zip(keep, got)]
    go = [add(k[n : 2 * n], g[n : 2 * n]) for k, g in zip(keep, got)]
    return stay, go


def split_low(keep, got):
    out = [
        jnp.stack([add(k[i : i + 1], g[i : i + 1]) for k, g in zip(keep, got)]) for i in range(4)
    ]
    return out[0], out[1:]


def last(keep, got):
    total = keep.astype(F32)
    for g in got:
        total = total + g.astype(F32)
    return total


def by_z(v, by):
    return (v, "expert", [(z, (z + by) % NZ) for z in range(NZ)])


def across_z(v, by):
    return (v, "expert", [(z, z ^ by) for z in range(NZ)])


def on_device(hidden, out_grad, gate_probs, expert_ids, base_down, delta_in, delta_out):
    tok, _, ff = hidden.shape
    width = out_grad.shape[1]
    rank = delta_in.shape[2]
    dp, own = lax.axis_index("dp"), lax.axis_index("expert")
    pos = lax.dynamic_index_in_dim(jnp.asarray(position_table()), dp, 0, keepdims=False)
    zpos = lax.dynamic_index_in_dim(jnp.asarray(z_table()), own, 0, keepdims=False)
    own = own.astype(jnp.int32).reshape(1)

    block = base_down.T.reshape(2, 1, 48, ff)
    got, (pos,), sent = exchange(low([block] * 3), [pos])
    held = merge_low([sent[0]] + got)
    rows, cols, coef_mine, ogt = front(pos, own, expert_ids.T, gate_probs.T, out_grad, delta_out)
    ogt = ogt.reshape(width, tok)
    hk = jnp.transpose(hidden, (1, 0, 2))
    hg = (gate_probs.T[:, :, None] * hk.astype(F32)).sum(axis=0).astype(BF)

    got, (own1,), sent = exchange(wide(held, 2) + [across_z(coef_mine, 1)], [own])
    held = merge([sent[:2], got[:2]])
    pair = jnp.stack([sent[2], got[2]])
    lat = latents(own1, rows, cols, hk, delta_in)

    got, (own2, lat), sent = exchange(wide(held, 3) + [by_z(pair, 2), by_z(pair, -2)], [own1, lat])
    w_own = merge_all(sent[:2], got[:2])
    pair = sent[2]
    back, ahead = got[2:]
    latent_b = lax.psum_scatter(lat, "expert", scatter_dimension=0, tiled=True)[0]
    send = base_part(own2, hg, ogt, 1)

    got, (own3,), sent = exchange(
        [core(w_own), core(send.reshape(2, 16, 48, ff)), by_z(back[:1], 2), by_z(ahead[1:], -2)],
        [own2],
    )
    base_keep = base_part(own3, hg, ogt, 0).reshape(2, 16, 48, ff)
    w_own, w_other = sent[0], got[0]
    coefs = jnp.concatenate([pair, back, ahead, got[2], got[3]], axis=0)
    base_keep, base_go = split(base_keep, got[1], 8)

    got, (zpos, own4), _ = exchange(wide(base_go, 3), [zpos, own3])
    in_keep, in_send, ct = delta_in_part(pos, zpos, cols, coefs, hk)
    base_keep, base_go = split(base_keep, got, 4)
    in_keep = in_keep.reshape(2, 16, 32, ff)

    got, (own5, latent_b), _ = exchange(
        wide(base_go, 2) + [core(in_send.reshape(2, 16, 32, ff))], [own4, latent_b]
    )
    gh, gg = back_pass(
        own5, cols, ogt, w_own.reshape(width // 2, ff), w_other.reshape(width // 2, ff), ct, delta_in, hk
    )
    out_keep, out_send = [
        v.reshape(2, 16, 48, rank) for v in delta_out_part(own5, cols, latent_b, ogt)
    ]
    base_keep, base_go = split_low(base_keep, got)
    in_keep, in_go = split(in_keep, got[2], 8)

    gg = gg.reshape(2, tok)
    got, _, sent = exchange(
        wide(in_go, 3) + [core(out_send), across_z(gg, 1)] + low(base_go), []
    )
    grad_hidden = jnp.transpose(gh, (1, 0, 2))
    grad_base = last(base_keep, got[4:]).reshape(96, ff).T
    in_keep, in_go = split(in_keep, got[:2], 4)
    gg = sent[3] + got[3]
    cut = [
        [add(out_keep[r, 4 * i : 4 * i + 4], got[2][r, 4 * i : 4 * i + 4]) for r in range(2)]
        for i in range(4)
    ]
    out_keep = jnp.stack(cut[0])
    out_go = [
        jnp.stack([cut[1][0], cut[2][1]]),
        jnp.stack([cut[2][0], cut[1][1]]),
        jnp.stack(cut[3]),
    ]

    got, _, sent = exchange(
        wide(in_go, 2)
        + [(v, "dp", step_pairs(0, *bits)) for v, bits in zip(out_go, ((2,), (3,), (2, 3)))]
        + [across_z(gg, 2)],
        [],
    )
    in_keep, in_go = split_low(in_keep, got)
    total = last(out_keep, got[2:5]).astype(BF)
    gg = sent[5] + got[5]

    got, _, sent = exchange(
        low(in_go) + low([total[:, i : i + 1] for i in (1, 2, 3)]) + [across_z(gg, 4)], []
    )
    grad_delta_in = jnp.transpose(last(in_keep, got[:3]).reshape(NZ, 8, ff), (0, 2, 1))
    grad_delta_out = last(total[:, :1], got[3:6]).reshape(96, rank).T[None]
    gg = sent[6] + got[6]
    return grad_hidden, gg.T, grad_base, grad_delta_in, grad_delta_out


def solution(mesh):
    in_specs = (
        P("dp", None, "expert"),
        P("dp", None),
        P("dp", None),
        P("dp", None),
        P("expert", "dp"),
        P(None, "expert", None),
        P("expert", None, None),
    )
    out_specs = (
        P("dp", None, "expert"),
        P("dp", None),
        P("expert", "dp"),
        P(None, "expert", "dp"),
        P("expert", None, "dp"),
    )
    return jax.shard_map(
        on_device, mesh=mesh, in_specs=in_specs, out_specs=out_specs, check_vma=False
    )
```

```python
import jax
import jax.numpy as jnp
import numpy as np
from jax import lax
from jax.experimental import pallas as pl
from jax.experimental.pallas import tpu as pltpu
from jax.sharding import PartitionSpec as P

BF = jnp.bfloat16
F32 = jnp.float32
NX = NY = 4
NZ = 8
NDP = 32
CAP = 192
VMEM = 50 * 1024 * 1024
CHEAP = pl.CostEstimate(flops=1000, bytes_accessed=1000, transcendentals=0)

SIDE_A = (1, 0, 3, 2)
SIDE_B = (3, 2, 1, 0)
GRAY = (0, 1, 3, 2)
LINKS = (
    (("yb", "ya", "xb", "xa"), ("yb", "ya", "xa", "xb")),
    (("xb", "xa", "yb", "ya"), ("xb", "xa", "ya", "yb")),
)


def dp_index(x, y, c):
    return (x * NY + y) * 2 + c


def neighbour(x, y, link):
    side = SIDE_A if link[1] == "a" else SIDE_B
    return (side[x], y) if link[0] == "x" else (x, side[y])


def step_pairs(stream, *bits):
    pairs = []
    for x in range(NX):
        for y in range(NY):
            for c in range(2):
                nx, ny = x, y
                for t in bits:
                    nx, ny = neighbour(nx, ny, LINKS[c][stream][t])
                pairs.append((dp_index(x, y, c), dp_index(nx, ny, c)))
    return pairs


CORE_PAIRS = [(i, i ^ 1) for i in range(NDP)]


def position_table():
    table = np.zeros((NDP, 2, NDP), np.int32)
    for x in range(NX):
        for y in range(NY):
            for c in range(2):
                for s in range(2):
                    for u in range(NX):
                        for v in range(NY):
                            for d in range(2):
                                differ = {
                                    "xa": (GRAY[x] ^ GRAY[u]) & 1,
                                    "xb": (GRAY[x] ^ GRAY[u]) >> 1,
                                    "ya": (GRAY[y] ^ GRAY[v]) & 1,
                                    "yb": (GRAY[y] ^ GRAY[v]) >> 1,
                                }
                                place = 16 * (c ^ d)
                                for t in range(4):
                                    place += differ[LINKS[d][s][t]] << t
                                table[dp_index(x, y, c), s, dp_index(u, v, d)] = place
    rows = 32 * (table // 16) + table % 16 + 16 * np.arange(2).reshape(1, 2, 1)
    return np.concatenate([rows.reshape(NDP, 2 * NDP), table.reshape(NDP, 2 * NDP)], axis=1).astype(np.int32)


def z_table():
    table = np.zeros((NZ, NZ), np.int32)
    for z in range(NZ):
        held = [z, z ^ 1]
        back, ahead = (z - 2) % NZ, (z + 2) % NZ
        far = (z + 4) % NZ
        held += [back, back ^ 1, ahead, ahead ^ 1, far, far ^ 1]
        for place, e in enumerate(held):
            table[z, e] = place
    return table


def params(**kw):
    return pltpu.CompilerParams(vmem_limit_bytes=VMEM, **kw)


def mm(a, b):
    return jnp.dot(a, b, preferred_element_type=F32)


def mm_nt(a, b):
    return lax.dot_general(a, b, (((1,), (1,)), ((), ())), preferred_element_type=F32)


def front_kernel(pos, own, ids_ref, gate_ref, og_ref, dout_ref, rows_ref, cols_ref, coef_ref, ogt_ref, acc):
    j = pl.program_id(0)
    tok = og_ref.shape[0]

    @pl.when(j == 0)
    def _():
        ids0, ids1 = ids_ref[0:1, :], ids_ref[1:2, :]
        g0, g1 = gate_ref[0:1, :], gate_ref[1:2, :]
        e = lax.broadcasted_iota(jnp.int32, (NZ, tok), 0)
        m0 = (e == ids0).astype(F32)
        m1 = (e == ids1).astype(F32)
        both = m0 + m1
        before = lax.broadcasted_iota(jnp.int32, (tok, tok), 0) < lax.broadcasted_iota(
            jnp.int32, (tok, tok), 1
        )
        rank = mm(both.astype(BF), before.astype(F32).astype(BF))
        rank = jnp.where(both > 0, rank, -1.0)
        rows_ref[...] = rank
        gates = m0 * g0 + m1 * g1
        ends = jnp.concatenate([g0, g1, jnp.zeros((6, tok), F32)], axis=0)
        wide = jnp.concatenate(
            [rank, m0, m1, gates, ends, jnp.zeros((88, tok), F32)], axis=0
        )
        cols_ref[...] = wide.T
        acc[...] = jnp.zeros_like(acc)

    og = og_ref[...]
    acc[...] += mm_nt(og, dout_ref[0])
    turned = og.T
    for b in range(4):
        for s in range(2):
            at = b * 96 + s * 48
            ogt_ref[pos[s * NDP + 4 * j + b]] = turned[at : at + 48]

    @pl.when(j == pl.num_programs(0) - 1)
    def _():
        rank = rows_ref[pl.ds(own[0], 1), :]
        slot = lax.broadcasted_iota(jnp.int32, (CAP, tok), 0).astype(F32)
        pick = (slot == rank).astype(F32).astype(BF)
        coef_ref[...] = mm(pick, acc[...].astype(BF)).astype(BF)


def front(pos, own, ids, gate, og, dout):
    tok, width = og.shape
    rank = dout.shape[1]
    chunk = 384
    return pl.pallas_call(
        front_kernel,
        out_shape=(
            jax.ShapeDtypeStruct((NZ, tok), F32),
            jax.ShapeDtypeStruct((tok, 128), F32),
            jax.ShapeDtypeStruct((CAP, rank), BF),
            jax.ShapeDtypeStruct((2 * NDP, 48, tok), BF),
        ),
        grid_spec=pltpu.PrefetchScalarGridSpec(
            num_scalar_prefetch=2,
            grid=(width // chunk,),
            in_specs=[
                pl.BlockSpec((2, tok), lambda j, p, o: (0, 0)),
                pl.BlockSpec((2, tok), lambda j, p, o: (0, 0)),
                pl.BlockSpec((tok, chunk), lambda j, p, o: (0, j)),
                pl.BlockSpec((1, rank, chunk), lambda j, p, o: (0, 0, j)),
            ],
            out_specs=[
                pl.BlockSpec((NZ, tok), lambda j, p, o: (0, 0)),
                pl.BlockSpec((tok, 128), lambda j, p, o: (0, 0)),
                pl.BlockSpec((CAP, rank), lambda j, p, o: (0, 0)),
                pl.BlockSpec((2 * NDP, 48, tok), lambda j, p, o: (0, 0, 0)),
            ],
            scratch_shapes=[pltpu.VMEM((tok, rank), F32)],
        ),
        compiler_params=params(),
        cost_estimate=CHEAP,
        name="front",
    )(pos, own, ids, gate, og, dout)


def chosen(h_ref, second):
    second = jnp.broadcast_to(second, h_ref.shape[1:]).astype(BF)
    return h_ref[0] * (1 - second) + h_ref[1] * second


def latent_kernel(zpos, rows_ref, cols_ref, h_ref, din_ref, out_ref):
    i = pl.program_id(0)
    tok = h_ref.shape[1]
    lane = lax.broadcasted_iota(jnp.int32, cols_ref.shape, 1)
    slot = lax.broadcasted_iota(jnp.int32, (CAP, tok), 0).astype(F32)
    for n in range(2):
        e = 2 * i + n
        second = jnp.sum(jnp.where(lane == 16 + e, cols_ref[...], 0.0), axis=1, keepdims=True)
        lat = mm(chosen(h_ref, second), din_ref[n]).astype(BF)
        pick = (slot == rows_ref[pl.ds(e, 1), :]).astype(F32).astype(BF)
        out_ref[zpos[e]] = mm(pick, lat).astype(BF)


def latents(zpos, rows, cols, hk, din):
    tok, ff = hk.shape[1:]
    rank = din.shape[2]
    return pl.pallas_call(
        latent_kernel,
        out_shape=jax.ShapeDtypeStruct((NZ, CAP, rank), BF),
        grid_spec=pltpu.PrefetchScalarGridSpec(
            num_scalar_prefetch=1,
            grid=(NZ // 2,),
            in_specs=[
                pl.BlockSpec((NZ, tok), lambda e, a: (0, 0)),
                pl.BlockSpec((tok, 128), lambda e, a: (0, 0)),
                pl.BlockSpec((2, tok, ff), lambda e, a: (0, 0, 0)),
                pl.BlockSpec((2, ff, rank), lambda e, a: (e, 0, 0)),
            ],
            out_specs=pl.BlockSpec((NZ, CAP, rank), lambda e, a: (0, 0, 0)),
        ),
        compiler_params=params(),
        cost_estimate=CHEAP,
        name="latents",
    )(zpos, rows, cols, hk, din)


def base_kernel(after, hg_ref, ogt_ref, out_ref):
    out_ref[...] = mm(ogt_ref[...], hg_ref[...]).astype(BF)


def base_part(after, hg, ogt, half):
    tok, ff = hg.shape
    rows = ogt.shape[0] // 2
    tile, steps = rows // 4, 4
    return pl.pallas_call(
        base_kernel,
        out_shape=jax.ShapeDtypeStruct((rows, ff), BF),
        grid_spec=pltpu.PrefetchScalarGridSpec(
            num_scalar_prefetch=1,
            grid=(steps,),
            in_specs=[
                pl.BlockSpec((tok, ff), lambda i, a: (0, 0)),
                pl.BlockSpec((tile, tok), lambda i, a: (i + steps * half, 0)),
            ],
            out_specs=pl.BlockSpec((tile, ff), lambda i, a: (i, 0)),
        ),
        compiler_params=params(),
        cost_estimate=CHEAP,
        name="base_part",
    )(after, hg, ogt)


def merge_kernel(*refs):
    count = len(refs) - 2
    for s in range(2):
        at = 0
        for p in range(count // 2):
            piece = refs[2 * p + s]
            n = piece.shape[0]
            refs[count + s][at : at + n] = piece[...]
            at += n


def merge(pieces):
    flat = [v for pair in pieces for v in pair]
    n = sum(pair[0].shape[0] for pair in pieces)
    out = jax.ShapeDtypeStruct((n,) + flat[0].shape[1:], BF)
    return pl.pallas_call(
        merge_kernel,
        out_shape=(out, out),
        compiler_params=params(),
        cost_estimate=CHEAP,
        name="merge",
    )(*flat)


def merge_low_kernel(a_ref, b_ref, c_ref, d_ref, first_ref, second_ref):
    for p, piece in enumerate((a_ref, b_ref, c_ref, d_ref)):
        first_ref[p] = piece[0, 0]
        second_ref[p] = piece[1, 0]


def merge_low(pieces):
    out = jax.ShapeDtypeStruct((4,) + pieces[0].shape[2:], BF)
    return pl.pallas_call(
        merge_low_kernel,
        out_shape=(out, out),
        compiler_params=params(),
        cost_estimate=CHEAP,
        name="merge_low",
    )(*pieces)


def merge_all_kernel(a0, a1, b0, b1, out_ref):
    for s, (a, b) in enumerate(((a0, b0), (a1, b1))):
        n = a.shape[0]
        out_ref[s, :n] = a[...]
        out_ref[s, n:] = b[...]


def merge_all(a, b):
    n = a[0].shape[0]
    return pl.pallas_call(
        merge_all_kernel,
        out_shape=jax.ShapeDtypeStruct((2, 2 * n) + a[0].shape[1:], BF),
        compiler_params=params(),
        cost_estimate=CHEAP,
        name="merge_all",
    )(*a, *b)


def column(cols, at):
    return cols[:, at : at + 1]


def delta_in_kernel(pos, zpos, cols_ref, ca_ref, cb_ref, h_ref, keep_ref, send_ref, ct_ref, turned):
    i = pl.program_id(0)
    s = i // 2
    tok = h_ref.shape[1]
    lane = lax.broadcasted_iota(jnp.int32, cols_ref.shape, 1)
    slot = lax.broadcasted_iota(jnp.int32, (tok, CAP), 1).astype(F32)
    parts = []
    for n, c_ref in enumerate((ca_ref, cb_ref)):
        e = 2 * i + n

        def col(base):
            return jnp.sum(jnp.where(lane == base + e, cols_ref[...], 0.0), axis=1, keepdims=True)

        spread = (slot == col(0)).astype(F32).astype(BF)
        coef = mm(spread, c_ref[0])
        ct_ref[n] = coef.astype(BF)
        weighted = (col(24) * coef).T
        for d in range(NDP):
            turned[pos[(2 + s) * NDP + d]] = weighted[8 * d : 8 * d + 8]
        w = turned[...].reshape(NDP * 8, tok).astype(BF)
        hid = chosen(h_ref, col(16))
        parts.append(mm(w, hid).reshape(NDP, 8, h_ref.shape[2]))
    both = jnp.concatenate(parts, axis=1).astype(BF)
    keep_ref[0, :, 0] = both[:16]
    send_ref[0, :, 0] = both[16:]


def delta_in_part(pos, zpos, cols, coefs, hk):
    tok, ff = hk.shape[1:]
    rank = coefs.shape[2]
    half = jax.ShapeDtypeStruct((2, 16, 2, 16, ff), BF)
    half_spec = pl.BlockSpec((1, 16, 1, 16, ff), lambda i, p, z: (i // 2, 0, i % 2, 0, 0))
    return pl.pallas_call(
        delta_in_kernel,
        out_shape=(half, half, jax.ShapeDtypeStruct((NZ, tok, rank), BF)),
        grid_spec=pltpu.PrefetchScalarGridSpec(
            num_scalar_prefetch=2,
            grid=(NZ // 2,),
            in_specs=[
                pl.BlockSpec((tok, 128), lambda i, p, z: (0, 0)),
                pl.BlockSpec((1, CAP, rank), lambda i, p, z: (z[2 * i], 0, 0)),
                pl.BlockSpec((1, CAP, rank), lambda i, p, z: (z[2 * i + 1], 0, 0)),
                pl.BlockSpec((2, tok, ff), lambda i, p, z: (0, 0, 0)),
            ],
            out_specs=[
                half_spec,
                half_spec,
                pl.BlockSpec((2, tok, rank), lambda i, p, z: (i, 0, 0)),
            ],
            scratch_shapes=[pltpu.VMEM((NDP, 8, tok), F32)],
        ),
        compiler_params=params(),
        cost_estimate=CHEAP,
        name="delta_in_part",
    )(pos, zpos, cols, coefs, coefs, hk)


def delta_out_kernel(own, cols_ref, lat_ref, keep_rows, send_rows, keep_ref, send_ref, spread):
    tok = cols_ref.shape[0]

    @pl.when(pl.program_id(0) == 0)
    def _():
        lane = lax.broadcasted_iota(jnp.int32, cols_ref.shape, 1)
        cols = cols_ref[...]
        rank = jnp.sum(jnp.where(lane == own[0], cols, 0.0), axis=1, keepdims=True)
        gate = jnp.sum(jnp.where(lane == 24 + own[0], cols, 0.0), axis=1, keepdims=True)
        slot = lax.broadcasted_iota(jnp.int32, (tok, CAP), 1).astype(F32)
        pick = (slot == rank).astype(F32).astype(BF)
        spread[...] = (gate * mm(pick, lat_ref[...])).astype(BF)

    keep_ref[...] = mm(keep_rows[...], spread[...]).astype(BF)
    send_ref[...] = mm(send_rows[...], spread[...]).astype(BF)


def delta_out_part(own, cols, lat, ogt):
    rows, tok = ogt.shape
    rank = lat.shape[1]
    tile = rows // 4
    half = jax.ShapeDtypeStruct((rows // 2, rank), BF)
    return pl.pallas_call(
        delta_out_kernel,
        out_shape=(half, half),
        grid_spec=pltpu.PrefetchScalarGridSpec(
            num_scalar_prefetch=1,
            grid=(2,),
            in_specs=[
                pl.BlockSpec((tok, 128), lambda i, o: (0, 0)),
                pl.BlockSpec((CAP, rank), lambda i, o: (0, 0)),
                pl.BlockSpec((tile, tok), lambda i, o: (i, 0)),
                pl.BlockSpec((tile, tok), lambda i, o: (i + 2, 0)),
            ],
            out_specs=[pl.BlockSpec((tile, rank), lambda i, o: (i, 0))] * 2,
            scratch_shapes=[pltpu.VMEM((tok, rank), BF)],
        ),
        compiler_params=params(),
        cost_estimate=CHEAP,
        name="delta_out_part",
    )(own, cols, lat, ogt, ogt)


def back_kernel(after, cols_ref, ogt_ref, w_own, w_other, ct_ref, din_ref, h_ref, gh_ref, gg_ref, og, lhs):
    n = pl.program_id(0)
    cols = cols_ref[...]
    quarter = ogt_ref.shape[0] // 4
    rank = ct_ref.shape[2]

    @pl.when(n == 0)
    def _():
        for a in range(4):
            og[:, a * quarter : (a + 1) * quarter] = ogt_ref[a * quarter : (a + 1) * quarter, :].T
        for e in range(NZ):
            coef = ct_ref[e].astype(F32)
            for k in range(2):
                lhs[k, :, e * rank : (e + 1) * rank] = (column(cols, 8 + 8 * k + e) * coef).astype(BF)
        gg_ref[...] = jnp.zeros_like(gg_ref)

    proj = mm(og[:, : 2 * quarter], w_own[...]) + mm(og[:, 2 * quarter :], w_other[...])
    for k in range(2):
        delta = mm_nt(lhs[k, :, :rank], din_ref[0])
        for e in range(1, NZ):
            delta = delta + mm_nt(lhs[k, :, e * rank : (e + 1) * rank], din_ref[e])
        back = proj + delta
        gh_ref[k] = (column(cols, 32 + k) * back).astype(BF)
        gg_ref[k] += jnp.sum(h_ref[k].astype(F32) * back, axis=1, keepdims=True)


def back_pass(after, cols, ogt, w_own, w_other, ct, din, hk):
    tok, ff = hk.shape[1:]
    rows = ogt.shape[0]
    rank = din.shape[2]
    tile = 256
    w_spec = pl.BlockSpec((rows // 2, tile), lambda n, a: (0, n))
    return pl.pallas_call(
        back_kernel,
        out_shape=(
            jax.ShapeDtypeStruct((2, tok, ff), BF),
            jax.ShapeDtypeStruct((2, tok, 1), F32),
        ),
        grid_spec=pltpu.PrefetchScalarGridSpec(
            num_scalar_prefetch=1,
            grid=(ff // tile,),
            in_specs=[
                pl.BlockSpec((tok, 128), lambda n, a: (0, 0)),
                pl.BlockSpec((rows, tok), lambda n, a: (0, 0)),
                w_spec,
                w_spec,
                pl.BlockSpec((NZ, tok, rank), lambda n, a: (0, 0, 0)),
                pl.BlockSpec((NZ, tile, rank), lambda n, a: (0, n, 0)),
                pl.BlockSpec((2, tok, tile), lambda n, a: (0, 0, n)),
            ],
            out_specs=[
                pl.BlockSpec((2, tok, tile), lambda n, a: (0, 0, n)),
                pl.BlockSpec((2, tok, 1), lambda n, a: (0, 0, 0)),
            ],
            scratch_shapes=[pltpu.VMEM((tok, rows), BF), pltpu.VMEM((2, tok, NZ * rank), BF)],
        ),
        compiler_params=params(),
        cost_estimate=CHEAP,
        name="back_pass",
    )(after, cols, ogt, w_own, w_other, ct, din, hk)


def add(a, b):
    return (a.astype(F32) + b.astype(F32)).astype(BF)


def tie_kernel(*refs):
    del refs


def tie(arrays):
    return pl.pallas_call(
        tie_kernel,
        out_shape=tuple(jax.ShapeDtypeStruct(v.shape, v.dtype) for v in arrays),
        in_specs=[pl.BlockSpec(memory_space=pl.ANY)] * len(arrays),
        out_specs=tuple(pl.BlockSpec(memory_space=pl.ANY) for _ in arrays),
        input_output_aliases={i: i for i in range(len(arrays))},
        compiler_params=pltpu.CompilerParams(has_side_effects=False, vmem_limit_bytes=1024 * 1024),
        cost_estimate=CHEAP,
        name="tie",
    )(*arrays)


def exchange(sends, pins):
    arrays, places = [], []
    for v in [v for v, _, _ in sends] + list(pins):
        same = [i for i, w in enumerate(arrays) if w is v]
        places.append(same[0] if same else len(arrays))
        if not same:
            arrays.append(v)
    tied = tie(arrays)
    tied = [tied[i] for i in places]
    got = [lax.ppermute(v, axis, pairs) for v, (_, axis, pairs) in zip(tied, sends)]
    return got, tied[len(sends) :], tied[: len(sends)]


def core(v):
    return (v, "dp", CORE_PAIRS)


def wide(sends, t):
    return [(sends[s], "dp", step_pairs(s, t)) for s in range(2)]


LOW = ((0,), (1,), (0, 1))


def low(blocks):
    return [(v, "dp", step_pairs(0, *bits)) for v, bits in zip(blocks, LOW)]


def split(keep, got, n):
    stay = [add(k[:n], g[:n]) for k, g in zip(keep, got)]
    go = [add(k[n : 2 * n], g[n : 2 * n]) for k, g in zip(keep, got)]
    return stay, go


def split_low(keep, got):
    out = [
        jnp.stack([add(k[i : i + 1], g[i : i + 1]) for k, g in zip(keep, got)]) for i in range(4)
    ]
    return out[0], out[1:]


def last(keep, got):
    total = keep.astype(F32)
    for g in got:
        total = total + g.astype(F32)
    return total


def by_z(v, by):
    return (v, "expert", [(z, (z + by) % NZ) for z in range(NZ)])


def across_z(v, by):
    return (v, "expert", [(z, z ^ by) for z in range(NZ)])


def on_device(hidden, out_grad, gate_probs, expert_ids, base_down, delta_in, delta_out):
    tok, _, ff = hidden.shape
    width = out_grad.shape[1]
    rank = delta_in.shape[2]
    dp, own = lax.axis_index("dp"), lax.axis_index("expert")
    pos = lax.dynamic_index_in_dim(jnp.asarray(position_table()), dp, 0, keepdims=False)
    zpos = lax.dynamic_index_in_dim(jnp.asarray(z_table()), own, 0, keepdims=False)
    own = own.astype(jnp.int32).reshape(1)

    block = base_down.T.reshape(2, 1, 48, ff)
    got, (pos,), sent = exchange(low([block] * 3), [pos])
    held = merge_low([sent[0]] + got)
    rows, cols, coef_mine, ogt = front(pos, own, expert_ids.T, gate_probs.T, out_grad, delta_out)
    ogt = ogt.reshape(width, tok)
    hk = jnp.transpose(hidden, (1, 0, 2))
    hg = (gate_probs.T[:, :, None] * hk.astype(F32)).sum(axis=0).astype(BF)

    got, (own1, zpos), sent = exchange(wide(held, 2) + [across_z(coef_mine, 1)], [own, zpos])
    held = merge([sent[:2], got[:2]])
    pair = jnp.stack([sent[2], got[2]])
    lat = latents(zpos, rows, cols, hk, delta_in)

    up = jnp.concatenate([pair, lat[6:7]], axis=0)
    down = jnp.concatenate([pair, lat[7:8]], axis=0)
    got, (own2,), sent = exchange(wide(held, 3) + [by_z(up, 2), by_z(down, -2)], [own1])
    w_own = merge_all(sent[:2], got[:2])
    back, ahead = got[2][:2], got[3][:2]
    up = jnp.concatenate([back[:1], add(lat[4:5], got[2][2:]), lat[5:6]], axis=0)
    down = jnp.concatenate([ahead[1:], lat[2:3], add(lat[3:4], got[3][2:])], axis=0)
    send = base_part(own2, hg, ogt, 1)

    got, (own3,), sent = exchange(
        [core(w_own), core(send.reshape(2, 16, 48, ff)), by_z(up, 2), by_z(down, -2)], [own2]
    )
    base_keep = base_part(own3, hg, ogt, 0).reshape(2, 16, 48, ff)
    w_own, w_other = sent[0], got[0]
    coefs = jnp.concatenate([pair, back, ahead, got[2][:1], got[3][:1]], axis=0)
    lat_mine, lat_mate = [last(lat[i], [got[2][1 + i], got[3][1 + i]]).astype(BF) for i in range(2)]
    base_keep, base_go = split(base_keep, got[1], 8)

    got, (own4, coefs), _ = exchange(wide(base_go, 3) + [across_z(lat_mate, 1)], [own3, coefs])
    latent_b = add(lat_mine, got[2])
    in_keep, in_send, ct = delta_in_part(pos, zpos, cols, coefs, hk)
    base_keep, base_go = split(base_keep, got, 4)
    in_keep = in_keep.reshape(2, 16, 32, ff)

    got, (own5, latent_b), _ = exchange(
        wide(base_go, 2) + [core(in_send.reshape(2, 16, 32, ff))], [own4, latent_b]
    )
    gh, gg = back_pass(
        own5, cols, ogt, w_own.reshape(width // 2, ff), w_other.reshape(width // 2, ff), ct, delta_in, hk
    )
    out_keep, out_send = [
        v.reshape(2, 16, 48, rank) for v in delta_out_part(own5, cols, latent_b, ogt)
    ]
    base_keep, base_go = split_low(base_keep, got)
    in_keep, in_go = split(in_keep, got[2], 8)

    gg = gg.reshape(2, tok)
    got, _, sent = exchange(
        wide(in_go, 3) + [core(out_send), across_z(gg, 1)] + low(base_go), []
    )
    grad_hidden = jnp.transpose(gh, (1, 0, 2))
    base_sum = last(base_keep, got[4:]).reshape(96, ff)
    in_keep, in_go = split(in_keep, got[:2], 4)
    gg = sent[3] + got[3]
    cut = [
        [add(out_keep[r, 4 * i : 4 * i + 4], got[2][r, 4 * i : 4 * i + 4]) for r in range(2)]
        for i in range(4)
    ]
    out_keep = jnp.stack(cut[0])
    out_go = [
        jnp.stack([cut[1][0], cut[2][1]]),
        jnp.stack([cut[2][0], cut[1][1]]),
        jnp.stack(cut[3]),
    ]

    got, (base_sum,), sent = exchange(
        wide(in_go, 2)
        + [(v, "dp", step_pairs(0, *bits)) for v, bits in zip(out_go, ((2,), (3,), (2, 3)))]
        + [across_z(gg, 2)],
        [base_sum],
    )
    grad_base = base_sum.T
    in_keep, in_go = split_low(in_keep, got)
    total = last(out_keep, got[2:5]).astype(BF)
    gg = sent[5] + got[5]

    got, _, sent = exchange(
        low(in_go) + low([total[:, i : i + 1] for i in (1, 2, 3)]) + [across_z(gg, 4)], []
    )
    grad_delta_in = jnp.transpose(last(in_keep, got[:3]).reshape(NZ, 8, ff), (0, 2, 1))
    grad_delta_out = last(total[:, :1], got[3:6]).reshape(96, rank).T[None]
    gg = sent[6] + got[6]
    return grad_hidden, gg.T, grad_base, grad_delta_in, grad_delta_out


def solution(mesh):
    in_specs = (
        P("dp", None, "expert"),
        P("dp", None),
        P("dp", None),
        P("dp", None),
        P("expert", "dp"),
        P(None, "expert", None),
        P("expert", None, None),
    )
    out_specs = (
        P("dp", None, "expert"),
        P("dp", None),
        P("expert", "dp"),
        P(None, "expert", "dp"),
        P("expert", None, "dp"),
    )
    return jax.shard_map(
        on_device, mesh=mesh, in_specs=in_specs, out_specs=out_specs, check_vma=False
    )
```

```python
import jax
import jax.numpy as jnp
import numpy as np
from jax import lax
from jax.experimental import pallas as pl
from jax.experimental.pallas import tpu as pltpu
from jax.sharding import PartitionSpec as P

BF = jnp.bfloat16
F32 = jnp.float32
NX = NY = 4
NZ = 8
NDP = 32
CAP = 192
MIB = 1024 * 1024
CHEAP = pl.CostEstimate(flops=1000, bytes_accessed=1000, transcendentals=0)

SIDE_A = (1, 0, 3, 2)
SIDE_B = (3, 2, 1, 0)
GRAY = (0, 1, 3, 2)
LINKS = (
    (("yb", "ya", "xb", "xa"), ("yb", "ya", "xa", "xb")),
    (("xb", "xa", "yb", "ya"), ("xb", "xa", "ya", "yb")),
)


def dp_index(x, y, c):
    return (x * NY + y) * 2 + c


def neighbour(x, y, link):
    side = SIDE_A if link[1] == "a" else SIDE_B
    return (side[x], y) if link[0] == "x" else (x, side[y])


def step_pairs(stream, *bits):
    pairs = []
    for x in range(NX):
        for y in range(NY):
            for c in range(2):
                nx, ny = x, y
                for t in bits:
                    nx, ny = neighbour(nx, ny, LINKS[c][stream][t])
                pairs.append((dp_index(x, y, c), dp_index(nx, ny, c)))
    return pairs


CORE_PAIRS = [(i, i ^ 1) for i in range(NDP)]


def position_table():
    table = np.zeros((NDP, 2, NDP), np.int32)
    for x in range(NX):
        for y in range(NY):
            for c in range(2):
                for s in range(2):
                    for u in range(NX):
                        for v in range(NY):
                            for d in range(2):
                                differ = {
                                    "xa": (GRAY[x] ^ GRAY[u]) & 1,
                                    "xb": (GRAY[x] ^ GRAY[u]) >> 1,
                                    "ya": (GRAY[y] ^ GRAY[v]) & 1,
                                    "yb": (GRAY[y] ^ GRAY[v]) >> 1,
                                }
                                place = 16 * (c ^ d)
                                for t in range(4):
                                    place += differ[LINKS[d][s][t]] << t
                                table[dp_index(x, y, c), s, dp_index(u, v, d)] = place
    rows = 32 * (table // 16) + table % 16 + 16 * np.arange(2).reshape(1, 2, 1)
    return np.concatenate([rows.reshape(NDP, 2 * NDP), table.reshape(NDP, 2 * NDP)], axis=1).astype(np.int32)


def z_table():
    table = np.zeros((NZ, NZ), np.int32)
    for z in range(NZ):
        held = [z, z ^ 1]
        back, ahead = (z - 2) % NZ, (z + 2) % NZ
        far = (z + 4) % NZ
        held += [back, back ^ 1, ahead, ahead ^ 1, far, far ^ 1]
        for place, e in enumerate(held):
            table[z, e] = place
    return table


def params(mib):
    return pltpu.CompilerParams(vmem_limit_bytes=mib * MIB)


def mm(a, b):
    return jnp.dot(a, b, preferred_element_type=F32)


def mm_nt(a, b):
    return lax.dot_general(a, b, (((1,), (1,)), ((), ())), preferred_element_type=F32)


def front_kernel(pos, own, ids_ref, gate_ref, og_ref, dout_ref, rows_ref, cols_ref, coef_ref, ogt_ref, acc):
    j = pl.program_id(0)
    tok = og_ref.shape[0]

    @pl.when(j == 0)
    def _():
        ids0, ids1 = ids_ref[0:1, :], ids_ref[1:2, :]
        g0, g1 = gate_ref[0:1, :], gate_ref[1:2, :]
        e = lax.broadcasted_iota(jnp.int32, (NZ, tok), 0)
        m0 = (e == ids0).astype(F32)
        m1 = (e == ids1).astype(F32)
        both = m0 + m1
        before = lax.broadcasted_iota(jnp.int32, (tok, tok), 0) < lax.broadcasted_iota(
            jnp.int32, (tok, tok), 1
        )
        rank = mm(both.astype(BF), before.astype(F32).astype(BF))
        rank = jnp.where(both > 0, rank, -1.0)
        rows_ref[...] = rank
        gates = m0 * g0 + m1 * g1
        ends = jnp.concatenate([g0, g1, jnp.zeros((6, tok), F32)], axis=0)
        wide = jnp.concatenate(
            [rank, m0, m1, gates, ends, jnp.zeros((88, tok), F32)], axis=0
        )
        cols_ref[...] = wide.T
        acc[...] = jnp.zeros_like(acc)

    og = og_ref[...]
    acc[...] += mm_nt(og, dout_ref[0])
    turned = og.T
    for b in range(4):
        for s in range(2):
            at = b * 96 + s * 48
            ogt_ref[pos[s * NDP + 4 * j + b]] = turned[at : at + 48]

    @pl.when(j == pl.num_programs(0) - 1)
    def _():
        rank = rows_ref[pl.ds(own[0], 1), :]
        slot = lax.broadcasted_iota(jnp.int32, (CAP, tok), 0).astype(F32)
        pick = (slot == rank).astype(F32).astype(BF)
        coef_ref[...] = mm(pick, acc[...].astype(BF)).astype(BF)


def front(pos, own, ids, gate, og, dout):
    tok, width = og.shape
    rank = dout.shape[1]
    chunk = 384
    return pl.pallas_call(
        front_kernel,
        out_shape=(
            jax.ShapeDtypeStruct((NZ, tok), F32),
            jax.ShapeDtypeStruct((tok, 128), F32),
            jax.ShapeDtypeStruct((CAP, rank), BF),
            jax.ShapeDtypeStruct((2 * NDP, 48, tok), BF),
        ),
        grid_spec=pltpu.PrefetchScalarGridSpec(
            num_scalar_prefetch=2,
            grid=(width // chunk,),
            in_specs=[
                pl.BlockSpec((2, tok), lambda j, p, o: (0, 0)),
                pl.BlockSpec((2, tok), lambda j, p, o: (0, 0)),
                pl.BlockSpec((tok, chunk), lambda j, p, o: (0, j)),
                pl.BlockSpec((1, rank, chunk), lambda j, p, o: (0, 0, j)),
            ],
            out_specs=[
                pl.BlockSpec((NZ, tok), lambda j, p, o: (0, 0)),
                pl.BlockSpec((tok, 128), lambda j, p, o: (0, 0)),
                pl.BlockSpec((CAP, rank), lambda j, p, o: (0, 0)),
                pl.BlockSpec((2 * NDP, 48, tok), lambda j, p, o: (0, 0, 0)),
            ],
            scratch_shapes=[pltpu.VMEM((tok, rank), F32)],
        ),
        compiler_params=params(20),
        cost_estimate=CHEAP,
        name="front",
    )(pos, own, ids, gate, og, dout)


def chosen(h_ref, second):
    second = jnp.broadcast_to(second, h_ref.shape[1:]).astype(BF)
    return h_ref[0] * (1 - second) + h_ref[1] * second


def latent_kernel(zpos, rows_ref, cols_ref, h_ref, din_ref, out_ref):
    i = pl.program_id(0)
    tok = h_ref.shape[1]
    lane = lax.broadcasted_iota(jnp.int32, cols_ref.shape, 1)
    slot = lax.broadcasted_iota(jnp.int32, (CAP, tok), 0).astype(F32)
    for n in range(2):
        e = 2 * i + n
        second = jnp.sum(jnp.where(lane == 16 + e, cols_ref[...], 0.0), axis=1, keepdims=True)
        lat = mm(chosen(h_ref, second), din_ref[n]).astype(BF)
        pick = (slot == rows_ref[pl.ds(e, 1), :]).astype(F32).astype(BF)
        out_ref[zpos[e]] = mm(pick, lat).astype(BF)


def latents(zpos, rows, cols, hk, din):
    tok, ff = hk.shape[1:]
    rank = din.shape[2]
    return pl.pallas_call(
        latent_kernel,
        out_shape=jax.ShapeDtypeStruct((NZ, CAP, rank), BF),
        grid_spec=pltpu.PrefetchScalarGridSpec(
            num_scalar_prefetch=1,
            grid=(NZ // 2,),
            in_specs=[
                pl.BlockSpec((NZ, tok), lambda e, a: (0, 0)),
                pl.BlockSpec((tok, 128), lambda e, a: (0, 0)),
                pl.BlockSpec((2, tok, ff), lambda e, a: (0, 0, 0)),
                pl.BlockSpec((2, ff, rank), lambda e, a: (e, 0, 0)),
            ],
            out_specs=pl.BlockSpec((NZ, CAP, rank), lambda e, a: (0, 0, 0)),
        ),
        compiler_params=params(20),
        cost_estimate=CHEAP,
        name="latents",
    )(zpos, rows, cols, hk, din)


def base_kernel(after, hg_ref, ogt_ref, out_ref):
    out_ref[...] = mm(ogt_ref[...], hg_ref[...]).astype(BF)


def base_part(after, hg, ogt, half):
    tok, ff = hg.shape
    rows = ogt.shape[0] // 2
    tile, steps = rows // 4, 4
    return pl.pallas_call(
        base_kernel,
        out_shape=jax.ShapeDtypeStruct((rows, ff), BF),
        grid_spec=pltpu.PrefetchScalarGridSpec(
            num_scalar_prefetch=1,
            grid=(steps,),
            in_specs=[
                pl.BlockSpec((tok, ff), lambda i, a: (0, 0)),
                pl.BlockSpec((tile, tok), lambda i, a: (i + steps * half, 0)),
            ],
            out_specs=pl.BlockSpec((tile, ff), lambda i, a: (i, 0)),
        ),
        compiler_params=params(16),
        cost_estimate=CHEAP,
        name="base_part",
    )(after, hg, ogt)


def merge_kernel(*refs):
    count = len(refs) - 2
    for s in range(2):
        at = 0
        for p in range(count // 2):
            piece = refs[2 * p + s]
            n = piece.shape[0]
            refs[count + s][at : at + n] = piece[...]
            at += n


def merge(pieces):
    flat = [v for pair in pieces for v in pair]
    n = sum(pair[0].shape[0] for pair in pieces)
    out = jax.ShapeDtypeStruct((n,) + flat[0].shape[1:], BF)
    return pl.pallas_call(
        merge_kernel,
        out_shape=(out, out),
        compiler_params=params(16),
        cost_estimate=CHEAP,
        name="merge",
    )(*flat)


def merge_low_kernel(a_ref, b_ref, c_ref, d_ref, first_ref, second_ref):
    for p, piece in enumerate((a_ref, b_ref, c_ref, d_ref)):
        first_ref[p] = piece[0, 0]
        second_ref[p] = piece[1, 0]


def merge_low(pieces):
    out = jax.ShapeDtypeStruct((4,) + pieces[0].shape[2:], BF)
    return pl.pallas_call(
        merge_low_kernel,
        out_shape=(out, out),
        compiler_params=params(12),
        cost_estimate=CHEAP,
        name="merge_low",
    )(*pieces)


def merge_all_kernel(a0, a1, b0, b1, out_ref):
    for s, (a, b) in enumerate(((a0, b0), (a1, b1))):
        n = a.shape[0]
        out_ref[s, :n] = a[...]
        out_ref[s, n:] = b[...]


def merge_all(a, b):
    n = a[0].shape[0]
    return pl.pallas_call(
        merge_all_kernel,
        out_shape=jax.ShapeDtypeStruct((2, 2 * n) + a[0].shape[1:], BF),
        compiler_params=params(20),
        cost_estimate=CHEAP,
        name="merge_all",
    )(*a, *b)


def column(cols, at):
    return cols[:, at : at + 1]


def delta_in_kernel(pos, zpos, cols_ref, ca_ref, cb_ref, h_ref, keep_ref, send_ref, ct_ref, turned):
    i = pl.program_id(0)
    s = i // 2
    tok = h_ref.shape[1]
    lane = lax.broadcasted_iota(jnp.int32, cols_ref.shape, 1)
    slot = lax.broadcasted_iota(jnp.int32, (tok, CAP), 1).astype(F32)
    parts = []
    for n, c_ref in enumerate((ca_ref, cb_ref)):
        e = 2 * i + n

        def col(base):
            return jnp.sum(jnp.where(lane == base + e, cols_ref[...], 0.0), axis=1, keepdims=True)

        spread = (slot == col(0)).astype(F32).astype(BF)
        coef = mm(spread, c_ref[0])
        ct_ref[n] = coef.astype(BF)
        weighted = (col(24) * coef).T
        for d in range(NDP):
            turned[pos[(2 + s) * NDP + d]] = weighted[8 * d : 8 * d + 8]
        w = turned[...].reshape(NDP * 8, tok).astype(BF)
        hid = chosen(h_ref, col(16))
        parts.append(mm(w, hid).reshape(NDP, 8, h_ref.shape[2]))
    both = jnp.concatenate(parts, axis=1).astype(BF)
    keep_ref[0, :, 0] = both[:16]
    send_ref[0, :, 0] = both[16:]


def delta_in_part(pos, zpos, cols, coefs, hk):
    tok, ff = hk.shape[1:]
    rank = coefs.shape[2]
    half = jax.ShapeDtypeStruct((2, 16, 2, 16, ff), BF)
    half_spec = pl.BlockSpec((1, 16, 1, 16, ff), lambda i, p, z: (i // 2, 0, i % 2, 0, 0))
    return pl.pallas_call(
        delta_in_kernel,
        out_shape=(half, half, jax.ShapeDtypeStruct((NZ, tok, rank), BF)),
        grid_spec=pltpu.PrefetchScalarGridSpec(
            num_scalar_prefetch=2,
            grid=(NZ // 2,),
            in_specs=[
                pl.BlockSpec((tok, 128), lambda i, p, z: (0, 0)),
                pl.BlockSpec((1, CAP, rank), lambda i, p, z: (z[2 * i], 0, 0)),
                pl.BlockSpec((1, CAP, rank), lambda i, p, z: (z[2 * i + 1], 0, 0)),
                pl.BlockSpec((2, tok, ff), lambda i, p, z: (0, 0, 0)),
            ],
            out_specs=[
                half_spec,
                half_spec,
                pl.BlockSpec((2, tok, rank), lambda i, p, z: (i, 0, 0)),
            ],
            scratch_shapes=[pltpu.VMEM((NDP, 8, tok), F32)],
        ),
        compiler_params=params(28),
        cost_estimate=CHEAP,
        name="delta_in_part",
    )(pos, zpos, cols, coefs, coefs, hk)


def delta_out_kernel(own, cols_ref, lat_ref, keep_rows, send_rows, keep_ref, send_ref, spread):
    tok = cols_ref.shape[0]

    @pl.when(pl.program_id(0) == 0)
    def _():
        lane = lax.broadcasted_iota(jnp.int32, cols_ref.shape, 1)
        cols = cols_ref[...]
        rank = jnp.sum(jnp.where(lane == own[0], cols, 0.0), axis=1, keepdims=True)
        gate = jnp.sum(jnp.where(lane == 24 + own[0], cols, 0.0), axis=1, keepdims=True)
        slot = lax.broadcasted_iota(jnp.int32, (tok, CAP), 1).astype(F32)
        pick = (slot == rank).astype(F32).astype(BF)
        spread[...] = (gate * mm(pick, lat_ref[...])).astype(BF)

    keep_ref[...] = mm(keep_rows[...], spread[...]).astype(BF)
    send_ref[...] = mm(send_rows[...], spread[...]).astype(BF)


def delta_out_part(own, cols, lat, ogt):
    rows, tok = ogt.shape
    rank = lat.shape[1]
    tile = rows // 4
    half = jax.ShapeDtypeStruct((rows // 2, rank), BF)
    return pl.pallas_call(
        delta_out_kernel,
        out_shape=(half, half),
        grid_spec=pltpu.PrefetchScalarGridSpec(
            num_scalar_prefetch=1,
            grid=(2,),
            in_specs=[
                pl.BlockSpec((tok, 128), lambda i, o: (0, 0)),
                pl.BlockSpec((CAP, rank), lambda i, o: (0, 0)),
                pl.BlockSpec((tile, tok), lambda i, o: (i, 0)),
                pl.BlockSpec((tile, tok), lambda i, o: (i + 2, 0)),
            ],
            out_specs=[pl.BlockSpec((tile, rank), lambda i, o: (i, 0))] * 2,
            scratch_shapes=[pltpu.VMEM((tok, rank), BF)],
        ),
        compiler_params=params(16),
        cost_estimate=CHEAP,
        name="delta_out_part",
    )(own, cols, lat, ogt, ogt)


def proj_kernel(after, ogt_ref, w_ref, out_ref, og):
    part = ogt_ref.shape[0] // 2

    @pl.when(pl.program_id(0) == 0)
    def _():
        for a in range(2):
            og[:, a * part : (a + 1) * part] = ogt_ref[a * part : (a + 1) * part, :].T

    out_ref[...] = mm(og[...], w_ref[...])


def proj_part(after, ogt, w):
    rows, tok = ogt.shape
    ff = w.shape[1]
    tile = 256
    return pl.pallas_call(
        proj_kernel,
        out_shape=jax.ShapeDtypeStruct((tok, ff), F32),
        grid_spec=pltpu.PrefetchScalarGridSpec(
            num_scalar_prefetch=1,
            grid=(ff // tile,),
            in_specs=[
                pl.BlockSpec((rows // 2, tok), lambda n, a: (0, 0)),
                pl.BlockSpec((rows // 2, tile), lambda n, a: (0, n)),
            ],
            out_specs=pl.BlockSpec((tok, tile), lambda n, a: (0, n)),
            scratch_shapes=[pltpu.VMEM((tok, rows // 2), BF)],
        ),
        compiler_params=params(16),
        cost_estimate=CHEAP,
        name="proj_part",
    )(after, ogt, w)


def back_kernel(after, cols_ref, ogt_ref, proj_ref, w_other, ct_ref, din_ref, h_ref, gh_ref, gg_ref, og, lhs):
    n = pl.program_id(0)
    cols = cols_ref[...]
    part = ogt_ref.shape[0] // 2
    rank = ct_ref.shape[2]

    @pl.when(n == 0)
    def _():
        for a in range(2):
            og[:, a * part : (a + 1) * part] = ogt_ref[a * part : (a + 1) * part, :].T
        for e in range(NZ):
            coef = ct_ref[e].astype(F32)
            for k in range(2):
                lhs[k, :, e * rank : (e + 1) * rank] = (column(cols, 8 + 8 * k + e) * coef).astype(BF)
        gg_ref[...] = jnp.zeros_like(gg_ref)

    proj = mm(og[...], w_other[...]) + proj_ref[...]
    for k in range(2):
        delta = mm_nt(lhs[k, :, :rank], din_ref[0])
        for e in range(1, NZ):
            delta = delta + mm_nt(lhs[k, :, e * rank : (e + 1) * rank], din_ref[e])
        back = proj + delta
        gh_ref[k] = (column(cols, 32 + k) * back).astype(BF)
        gg_ref[k] += jnp.sum(h_ref[k].astype(F32) * back, axis=1, keepdims=True)


def back_pass(after, cols, ogt, proj, w_other, ct, din, hk):
    tok, ff = hk.shape[1:]
    rows = ogt.shape[0]
    rank = din.shape[2]
    tile = 256
    w_spec = pl.BlockSpec((rows // 2, tile), lambda n, a: (0, n))
    return pl.pallas_call(
        back_kernel,
        out_shape=(
            jax.ShapeDtypeStruct((2, tok, ff), BF),
            jax.ShapeDtypeStruct((2, tok, 1), F32),
        ),
        grid_spec=pltpu.PrefetchScalarGridSpec(
            num_scalar_prefetch=1,
            grid=(ff // tile,),
            in_specs=[
                pl.BlockSpec((tok, 128), lambda n, a: (0, 0)),
                pl.BlockSpec((rows // 2, tok), lambda n, a: (1, 0)),
                pl.BlockSpec((tok, tile), lambda n, a: (0, n)),
                w_spec,
                pl.BlockSpec((NZ, tok, rank), lambda n, a: (0, 0, 0)),
                pl.BlockSpec((NZ, tile, rank), lambda n, a: (0, n, 0)),
                pl.BlockSpec((2, tok, tile), lambda n, a: (0, 0, n)),
            ],
            out_specs=[
                pl.BlockSpec((2, tok, tile), lambda n, a: (0, 0, n)),
                pl.BlockSpec((2, tok, 1), lambda n, a: (0, 0, 0)),
            ],
            scratch_shapes=[pltpu.VMEM((tok, rows // 2), BF), pltpu.VMEM((2, tok, NZ * rank), BF)],
        ),
        compiler_params=params(36),
        cost_estimate=CHEAP,
        name="back_pass",
    )(after, cols, ogt, proj, w_other, ct, din, hk)


def add(a, b):
    return (a.astype(F32) + b.astype(F32)).astype(BF)


def tie_kernel(*refs):
    del refs


def tie(arrays):
    return pl.pallas_call(
        tie_kernel,
        out_shape=tuple(jax.ShapeDtypeStruct(v.shape, v.dtype) for v in arrays),
        in_specs=[pl.BlockSpec(memory_space=pl.ANY)] * len(arrays),
        out_specs=tuple(pl.BlockSpec(memory_space=pl.ANY) for _ in arrays),
        input_output_aliases={i: i for i in range(len(arrays))},
        compiler_params=pltpu.CompilerParams(has_side_effects=False, vmem_limit_bytes=1024 * 1024),
        cost_estimate=CHEAP,
        name="tie",
    )(*arrays)


def exchange(sends, pins):
    arrays, places = [], []
    for v in [v for v, _, _ in sends] + list(pins):
        same = [i for i, w in enumerate(arrays) if w is v]
        places.append(same[0] if same else len(arrays))
        if not same:
            arrays.append(v)
    tied = tie(arrays)
    tied = [tied[i] for i in places]
    got = [lax.ppermute(v, axis, pairs) for v, (_, axis, pairs) in zip(tied, sends)]
    return got, tied[len(sends) :], tied[: len(sends)]


def core(v):
    return (v, "dp", CORE_PAIRS)


def wide(sends, t):
    return [(sends[s], "dp", step_pairs(s, t)) for s in range(2)]


LOW = ((0,), (1,), (0, 1))


def low(blocks):
    return [(v, "dp", step_pairs(0, *bits)) for v, bits in zip(blocks, LOW)]


def split(keep, got, n):
    stay = [add(k[:n], g[:n]) for k, g in zip(keep, got)]
    go = [add(k[n : 2 * n], g[n : 2 * n]) for k, g in zip(keep, got)]
    return stay, go


def split_low(keep, got):
    out = [
        jnp.stack([add(k[i : i + 1], g[i : i + 1]) for k, g in zip(keep, got)]) for i in range(4)
    ]
    return out[0], out[1:]


def last(keep, got):
    total = keep.astype(F32)
    for g in got:
        total = total + g.astype(F32)
    return total


def by_z(v, by):
    return (v, "expert", [(z, (z + by) % NZ) for z in range(NZ)])


def across_z(v, by):
    return (v, "expert", [(z, z ^ by) for z in range(NZ)])


def on_device(hidden, out_grad, gate_probs, expert_ids, base_down, delta_in, delta_out):
    tok, _, ff = hidden.shape
    width = out_grad.shape[1]
    rank = delta_in.shape[2]
    dp, own = lax.axis_index("dp"), lax.axis_index("expert")
    pos = lax.dynamic_index_in_dim(jnp.asarray(position_table()), dp, 0, keepdims=False)
    zpos = lax.dynamic_index_in_dim(jnp.asarray(z_table()), own, 0, keepdims=False)
    own = own.astype(jnp.int32).reshape(1)

    block = base_down.T.reshape(2, 1, 48, ff)
    got, (pos,), sent = exchange(low([block] * 3), [pos])
    held = merge_low([sent[0]] + got)
    rows, cols, coef_mine, ogt = front(pos, own, expert_ids.T, gate_probs.T, out_grad, delta_out)
    ogt = ogt.reshape(width, tok)
    hk = jnp.transpose(hidden, (1, 0, 2))
    hg = (gate_probs.T[:, :, None] * hk.astype(F32)).sum(axis=0).astype(BF)

    got, (own1, zpos), sent = exchange(wide(held, 2) + [across_z(coef_mine, 1)], [own, zpos])
    held = merge([sent[:2], got[:2]])
    pair = jnp.stack([sent[2], got[2]])
    lat = latents(zpos, rows, cols, hk, delta_in)

    up = jnp.concatenate([pair, lat[6:7]], axis=0)
    down = jnp.concatenate([pair, lat[7:8]], axis=0)
    got, (own2,), sent = exchange(wide(held, 3) + [by_z(up, 2), by_z(down, -2)], [own1])
    w_own = merge_all(sent[:2], got[:2])
    back, ahead = got[2][:2], got[3][:2]
    up = jnp.concatenate([back[:1], add(lat[4:5], got[2][2:]), lat[5:6]], axis=0)
    down = jnp.concatenate([ahead[1:], lat[2:3], add(lat[3:4], got[3][2:])], axis=0)
    send = base_part(own2, hg, ogt, 1)

    got, (own3,), sent = exchange(
        [core(w_own), core(send.reshape(2, 16, 48, ff)), by_z(up, 2), by_z(down, -2)], [own2]
    )
    base_keep = base_part(own3, hg, ogt, 0).reshape(2, 16, 48, ff)
    w_other = got[0]
    proj = proj_part(own3, ogt, sent[0].reshape(width // 2, ff))
    coefs = jnp.concatenate([pair, back, ahead, got[2][:1], got[3][:1]], axis=0)
    lat_mine, lat_mate = [last(lat[i], [got[2][1 + i], got[3][1 + i]]).astype(BF) for i in range(2)]
    base_keep, base_go = split(base_keep, got[1], 8)

    got, (own4, coefs, proj), _ = exchange(
        wide(base_go, 3) + [across_z(lat_mate, 1)], [own3, coefs, proj]
    )
    latent_b = add(lat_mine, got[2])
    in_keep, in_send, ct = delta_in_part(pos, zpos, cols, coefs, hk)
    base_keep, base_go = split(base_keep, got, 4)
    in_keep = in_keep.reshape(2, 16, 32, ff)

    got, (own5, latent_b), _ = exchange(
        wide(base_go, 2) + [core(in_send.reshape(2, 16, 32, ff))], [own4, latent_b]
    )
    gh, gg = back_pass(
        own5, cols, ogt, proj, w_other.reshape(width // 2, ff), ct, delta_in, hk
    )
    out_keep, out_send = [
        v.reshape(2, 16, 48, rank) for v in delta_out_part(own5, cols, latent_b, ogt)
    ]
    base_keep, base_go = split_low(base_keep, got)
    in_keep, in_go = split(in_keep, got[2], 8)

    gg = gg.reshape(2, tok)
    got, _, sent = exchange(
        wide(in_go, 3) + [core(out_send), across_z(gg, 1)] + low(base_go), []
    )
    grad_hidden = jnp.transpose(gh, (1, 0, 2))
    grad_base = last(base_keep, got[4:]).reshape(96, ff).T
    in_keep, in_go = split(in_keep, got[:2], 4)
    gg = sent[3] + got[3]
    cut = [
        [add(out_keep[r, 4 * i : 4 * i + 4], got[2][r, 4 * i : 4 * i + 4]) for r in range(2)]
        for i in range(4)
    ]
    out_keep = jnp.stack(cut[0])
    out_go = [
        jnp.stack([cut[1][0], cut[2][1]]),
        jnp.stack([cut[2][0], cut[1][1]]),
        jnp.stack(cut[3]),
    ]

    got, _, sent = exchange(
        wide(in_go, 2)
        + [(v, "dp", step_pairs(0, *bits)) for v, bits in zip(out_go, ((2,), (3,), (2, 3)))]
        + [across_z(gg, 2)],
        [],
    )
    in_keep, in_go = split_low(in_keep, got)
    total = last(out_keep, got[2:5]).astype(BF)
    gg = sent[5] + got[5]

    got, _, sent = exchange(
        low(in_go) + low([total[:, i : i + 1] for i in (1, 2, 3)]) + [across_z(gg, 4)], []
    )
    grad_delta_in = jnp.transpose(last(in_keep, got[:3]).reshape(NZ, 8, ff), (0, 2, 1))
    grad_delta_out = last(total[:, :1], got[3:6]).reshape(96, rank).T[None]
    gg = sent[6] + got[6]
    return grad_hidden, gg.T, grad_base, grad_delta_in, grad_delta_out


def solution(mesh):
    in_specs = (
        P("dp", None, "expert"),
        P("dp", None),
        P("dp", None),
        P("dp", None),
        P("expert", "dp"),
        P(None, "expert", None),
        P("expert", None, None),
    )
    out_specs = (
        P("dp", None, "expert"),
        P("dp", None),
        P("expert", "dp"),
        P(None, "expert", "dp"),
        P("expert", None, "dp"),
    )
    return jax.shard_map(
        on_device, mesh=mesh, in_specs=in_specs, out_specs=out_specs, check_vma=False
    )
```

```python
import jax
import jax.numpy as jnp
import numpy as np
from jax import lax
from jax.experimental import pallas as pl
from jax.experimental.pallas import tpu as pltpu
from jax.sharding import PartitionSpec as P

BF = jnp.bfloat16
F32 = jnp.float32
NX = NY = 4
NZ = 8
NDP = 32
CAP = 192
MIB = 1024 * 1024
CHEAP = pl.CostEstimate(flops=1000, bytes_accessed=1000, transcendentals=0)

SIDE_A = (1, 0, 3, 2)
SIDE_B = (3, 2, 1, 0)
GRAY = (0, 1, 3, 2)
LINKS = (
    (("yb", "ya", "xb", "xa"), ("yb", "ya", "xa", "xb")),
    (("xb", "xa", "yb", "ya"), ("xb", "xa", "ya", "yb")),
)


def dp_index(x, y, c):
    return (x * NY + y) * 2 + c


def neighbour(x, y, link):
    side = SIDE_A if link[1] == "a" else SIDE_B
    return (side[x], y) if link[0] == "x" else (x, side[y])


def step_pairs(stream, *bits):
    pairs = []
    for x in range(NX):
        for y in range(NY):
            for c in range(2):
                nx, ny = x, y
                for t in bits:
                    nx, ny = neighbour(nx, ny, LINKS[c][stream][t])
                pairs.append((dp_index(x, y, c), dp_index(nx, ny, c)))
    return pairs


CORE_PAIRS = [(i, i ^ 1) for i in range(NDP)]


def position_table():
    table = np.zeros((NDP, 2, NDP), np.int32)
    for x in range(NX):
        for y in range(NY):
            for c in range(2):
                for s in range(2):
                    for u in range(NX):
                        for v in range(NY):
                            for d in range(2):
                                differ = {
                                    "xa": (GRAY[x] ^ GRAY[u]) & 1,
                                    "xb": (GRAY[x] ^ GRAY[u]) >> 1,
                                    "ya": (GRAY[y] ^ GRAY[v]) & 1,
                                    "yb": (GRAY[y] ^ GRAY[v]) >> 1,
                                }
                                place = 16 * (c ^ d)
                                for t in range(4):
                                    place += differ[LINKS[d][s][t]] << t
                                table[dp_index(x, y, c), s, dp_index(u, v, d)] = place
    rows = 32 * (table // 16) + table % 16 + 16 * np.arange(2).reshape(1, 2, 1)
    return np.concatenate([rows.reshape(NDP, 2 * NDP), table.reshape(NDP, 2 * NDP)], axis=1).astype(np.int32)


def z_table():
    table = np.zeros((NZ, NZ), np.int32)
    for z in range(NZ):
        held = [z, z ^ 1]
        back, ahead = (z - 2) % NZ, (z + 2) % NZ
        far = (z + 4) % NZ
        held += [back, back ^ 1, ahead, ahead ^ 1, far, far ^ 1]
        for place, e in enumerate(held):
            table[z, e] = place
    return table


def params(mib):
    return pltpu.CompilerParams(vmem_limit_bytes=mib * MIB)


def mm(a, b):
    return jnp.dot(a, b, preferred_element_type=F32)


def mm_nt(a, b):
    return lax.dot_general(a, b, (((1,), (1,)), ((), ())), preferred_element_type=F32)


def front_kernel(pos, own, ids_ref, gate_ref, og_ref, dout_ref, rows_ref, cols_ref, coef_ref, ogt_ref, acc):
    j = pl.program_id(0)
    tok = og_ref.shape[0]

    @pl.when(j == 0)
    def _():
        ids0, ids1 = ids_ref[0:1, :], ids_ref[1:2, :]
        g0, g1 = gate_ref[0:1, :], gate_ref[1:2, :]
        e = lax.broadcasted_iota(jnp.int32, (NZ, tok), 0)
        m0 = (e == ids0).astype(F32)
        m1 = (e == ids1).astype(F32)
        both = m0 + m1
        before = lax.broadcasted_iota(jnp.int32, (tok, tok), 0) < lax.broadcasted_iota(
            jnp.int32, (tok, tok), 1
        )
        rank = mm(both.astype(BF), before.astype(F32).astype(BF))
        rank = jnp.where(both > 0, rank, -1.0)
        rows_ref[...] = rank
        gates = m0 * g0 + m1 * g1
        ends = jnp.concatenate([g0, g1, jnp.zeros((6, tok), F32)], axis=0)
        wide = jnp.concatenate(
            [rank, m0, m1, gates, ends, jnp.zeros((88, tok), F32)], axis=0
        )
        cols_ref[...] = wide.T
        acc[...] = jnp.zeros_like(acc)

    og = og_ref[...]
    acc[...] += mm_nt(og, dout_ref[0])
    turned = og.T
    for b in range(4):
        for s in range(2):
            at = b * 96 + s * 48
            ogt_ref[pos[s * NDP + 4 * j + b]] = turned[at : at + 48]

    @pl.when(j == pl.num_programs(0) - 1)
    def _():
        rank = rows_ref[pl.ds(own[0], 1), :]
        slot = lax.broadcasted_iota(jnp.int32, (CAP, tok), 0).astype(F32)
        pick = (slot == rank).astype(F32).astype(BF)
        coef_ref[...] = mm(pick, acc[...].astype(BF)).astype(BF)


def front(pos, own, ids, gate, og, dout):
    tok, width = og.shape
    rank = dout.shape[1]
    chunk = 384
    return pl.pallas_call(
        front_kernel,
        out_shape=(
            jax.ShapeDtypeStruct((NZ, tok), F32),
            jax.ShapeDtypeStruct((tok, 128), F32),
            jax.ShapeDtypeStruct((CAP, rank), BF),
            jax.ShapeDtypeStruct((2 * NDP, 48, tok), BF),
        ),
        grid_spec=pltpu.PrefetchScalarGridSpec(
            num_scalar_prefetch=2,
            grid=(width // chunk,),
            in_specs=[
                pl.BlockSpec((2, tok), lambda j, p, o: (0, 0)),
                pl.BlockSpec((2, tok), lambda j, p, o: (0, 0)),
                pl.BlockSpec((tok, chunk), lambda j, p, o: (0, j)),
                pl.BlockSpec((1, rank, chunk), lambda j, p, o: (0, 0, j)),
            ],
            out_specs=[
                pl.BlockSpec((NZ, tok), lambda j, p, o: (0, 0)),
                pl.BlockSpec((tok, 128), lambda j, p, o: (0, 0)),
                pl.BlockSpec((CAP, rank), lambda j, p, o: (0, 0)),
                pl.BlockSpec((2 * NDP, 48, tok), lambda j, p, o: (0, 0, 0)),
            ],
            scratch_shapes=[pltpu.VMEM((tok, rank), F32)],
        ),
        compiler_params=params(20),
        cost_estimate=CHEAP,
        name="front",
    )(pos, own, ids, gate, og, dout)


def chosen(h_ref, second):
    second = jnp.broadcast_to(second, h_ref.shape[1:]).astype(BF)
    return h_ref[0] * (1 - second) + h_ref[1] * second


def latent_kernel(zpos, rows_ref, cols_ref, h_ref, din_ref, out_ref):
    i = pl.program_id(0)
    tok = h_ref.shape[1]
    lane = lax.broadcasted_iota(jnp.int32, cols_ref.shape, 1)
    slot = lax.broadcasted_iota(jnp.int32, (CAP, tok), 0).astype(F32)
    for n in range(2):
        e = 2 * i + n
        second = jnp.sum(jnp.where(lane == 16 + e, cols_ref[...], 0.0), axis=1, keepdims=True)
        lat = mm(chosen(h_ref, second), din_ref[n]).astype(BF)
        pick = (slot == rows_ref[pl.ds(e, 1), :]).astype(F32).astype(BF)
        out_ref[zpos[e]] = mm(pick, lat).astype(BF)


def latents(zpos, rows, cols, hk, din):
    tok, ff = hk.shape[1:]
    rank = din.shape[2]
    return pl.pallas_call(
        latent_kernel,
        out_shape=jax.ShapeDtypeStruct((NZ, CAP, rank), BF),
        grid_spec=pltpu.PrefetchScalarGridSpec(
            num_scalar_prefetch=1,
            grid=(NZ // 2,),
            in_specs=[
                pl.BlockSpec((NZ, tok), lambda e, a: (0, 0)),
                pl.BlockSpec((tok, 128), lambda e, a: (0, 0)),
                pl.BlockSpec((2, tok, ff), lambda e, a: (0, 0, 0)),
                pl.BlockSpec((2, ff, rank), lambda e, a: (e, 0, 0)),
            ],
            out_specs=pl.BlockSpec((NZ, CAP, rank), lambda e, a: (0, 0, 0)),
        ),
        compiler_params=params(20),
        cost_estimate=CHEAP,
        name="latents",
    )(zpos, rows, cols, hk, din)


def base_kernel(after, hg_ref, ogt_ref, out_ref):
    out_ref[...] = mm(ogt_ref[...], hg_ref[...]).astype(BF)


def base_part(after, hg, ogt, half):
    tok, ff = hg.shape
    rows = ogt.shape[0] // 2
    tile, steps = rows // 4, 4
    return pl.pallas_call(
        base_kernel,
        out_shape=jax.ShapeDtypeStruct((rows, ff), BF),
        grid_spec=pltpu.PrefetchScalarGridSpec(
            num_scalar_prefetch=1,
            grid=(steps,),
            in_specs=[
                pl.BlockSpec((tok, ff), lambda i, a: (0, 0)),
                pl.BlockSpec((tile, tok), lambda i, a: (i + steps * half, 0)),
            ],
            out_specs=pl.BlockSpec((tile, ff), lambda i, a: (i, 0)),
        ),
        compiler_params=params(16),
        cost_estimate=CHEAP,
        name="base_part",
    )(after, hg, ogt)


def merge_kernel(*refs):
    count = len(refs) - 2
    for s in range(2):
        at = 0
        for p in range(count // 2):
            piece = refs[2 * p + s]
            n = piece.shape[0]
            refs[count + s][at : at + n] = piece[...]
            at += n


def merge(pieces):
    flat = [v for pair in pieces for v in pair]
    n = sum(pair[0].shape[0] for pair in pieces)
    out = jax.ShapeDtypeStruct((n,) + flat[0].shape[1:], BF)
    return pl.pallas_call(
        merge_kernel,
        out_shape=(out, out),
        compiler_params=params(16),
        cost_estimate=CHEAP,
        name="merge",
    )(*flat)


def merge_low_kernel(a_ref, b_ref, c_ref, d_ref, first_ref, second_ref):
    for p, piece in enumerate((a_ref, b_ref, c_ref, d_ref)):
        first_ref[p] = piece[0, 0]
        second_ref[p] = piece[1, 0]


def merge_low(pieces):
    out = jax.ShapeDtypeStruct((4,) + pieces[0].shape[2:], BF)
    return pl.pallas_call(
        merge_low_kernel,
        out_shape=(out, out),
        compiler_params=params(12),
        cost_estimate=CHEAP,
        name="merge_low",
    )(*pieces)


def merge_all_kernel(a0, a1, b0, b1, out_ref):
    for s, (a, b) in enumerate(((a0, b0), (a1, b1))):
        n = a.shape[0]
        out_ref[s, :n] = a[...]
        out_ref[s, n:] = b[...]


def merge_all(a, b):
    n = a[0].shape[0]
    return pl.pallas_call(
        merge_all_kernel,
        out_shape=jax.ShapeDtypeStruct((2, 2 * n) + a[0].shape[1:], BF),
        compiler_params=params(20),
        cost_estimate=CHEAP,
        name="merge_all",
    )(*a, *b)


def column(cols, at):
    return cols[:, at : at + 1]


def delta_in_kernel(pos, zpos, cols_ref, ca_ref, cb_ref, h_ref, keep_ref, send_ref, ct_ref, turned):
    i = pl.program_id(0)
    s = i // 2
    tok = h_ref.shape[1]
    lane = lax.broadcasted_iota(jnp.int32, cols_ref.shape, 1)
    slot = lax.broadcasted_iota(jnp.int32, (tok, CAP), 1).astype(F32)
    parts = []
    for n, c_ref in enumerate((ca_ref, cb_ref)):
        e = 2 * i + n

        def col(base):
            return jnp.sum(jnp.where(lane == base + e, cols_ref[...], 0.0), axis=1, keepdims=True)

        spread = (slot == col(0)).astype(F32).astype(BF)
        coef = mm(spread, c_ref[0])
        ct_ref[n] = coef.astype(BF)
        weighted = (col(24) * coef).T
        for d in range(NDP):
            turned[pos[(2 + s) * NDP + d]] = weighted[8 * d : 8 * d + 8]
        w = turned[...].reshape(NDP * 8, tok).astype(BF)
        hid = chosen(h_ref, col(16))
        parts.append(mm(w, hid).reshape(NDP, 8, h_ref.shape[2]))
    both = jnp.concatenate(parts, axis=1).astype(BF)
    keep_ref[0, :, 0] = both[:16]
    send_ref[0, :, 0] = both[16:]


def delta_in_part(pos, zpos, cols, coefs, hk):
    tok, ff = hk.shape[1:]
    rank = coefs.shape[2]
    half = jax.ShapeDtypeStruct((2, 16, 2, 16, ff), BF)
    half_spec = pl.BlockSpec((1, 16, 1, 16, ff), lambda i, p, z: (i // 2, 0, i % 2, 0, 0))
    return pl.pallas_call(
        delta_in_kernel,
        out_shape=(half, half, jax.ShapeDtypeStruct((NZ, tok, rank), BF)),
        grid_spec=pltpu.PrefetchScalarGridSpec(
            num_scalar_prefetch=2,
            grid=(NZ // 2,),
            in_specs=[
                pl.BlockSpec((tok, 128), lambda i, p, z: (0, 0)),
                pl.BlockSpec((1, CAP, rank), lambda i, p, z: (z[2 * i], 0, 0)),
                pl.BlockSpec((1, CAP, rank), lambda i, p, z: (z[2 * i + 1], 0, 0)),
                pl.BlockSpec((2, tok, ff), lambda i, p, z: (0, 0, 0)),
            ],
            out_specs=[
                half_spec,
                half_spec,
                pl.BlockSpec((2, tok, rank), lambda i, p, z: (i, 0, 0)),
            ],
            scratch_shapes=[pltpu.VMEM((NDP, 8, tok), F32)],
        ),
        compiler_params=params(28),
        cost_estimate=CHEAP,
        name="delta_in_part",
    )(pos, zpos, cols, coefs, coefs, hk)


def delta_out_kernel(own, cols_ref, lat_ref, keep_rows, send_rows, keep_ref, send_ref, spread):
    tok = cols_ref.shape[0]

    @pl.when(pl.program_id(0) == 0)
    def _():
        lane = lax.broadcasted_iota(jnp.int32, cols_ref.shape, 1)
        cols = cols_ref[...]
        rank = jnp.sum(jnp.where(lane == own[0], cols, 0.0), axis=1, keepdims=True)
        gate = jnp.sum(jnp.where(lane == 24 + own[0], cols, 0.0), axis=1, keepdims=True)
        slot = lax.broadcasted_iota(jnp.int32, (tok, CAP), 1).astype(F32)
        pick = (slot == rank).astype(F32).astype(BF)
        spread[...] = (gate * mm(pick, lat_ref[...])).astype(BF)

    keep_ref[...] = mm(keep_rows[...], spread[...]).astype(BF)
    send_ref[...] = mm(send_rows[...], spread[...]).astype(BF)


def delta_out_part(own, cols, lat, ogt):
    rows, tok = ogt.shape
    rank = lat.shape[1]
    tile = rows // 4
    half = jax.ShapeDtypeStruct((rows // 2, rank), BF)
    return pl.pallas_call(
        delta_out_kernel,
        out_shape=(half, half),
        grid_spec=pltpu.PrefetchScalarGridSpec(
            num_scalar_prefetch=1,
            grid=(2,),
            in_specs=[
                pl.BlockSpec((tok, 128), lambda i, o: (0, 0)),
                pl.BlockSpec((CAP, rank), lambda i, o: (0, 0)),
                pl.BlockSpec((tile, tok), lambda i, o: (i, 0)),
                pl.BlockSpec((tile, tok), lambda i, o: (i + 2, 0)),
            ],
            out_specs=[pl.BlockSpec((tile, rank), lambda i, o: (i, 0))] * 2,
            scratch_shapes=[pltpu.VMEM((tok, rank), BF)],
        ),
        compiler_params=params(16),
        cost_estimate=CHEAP,
        name="delta_out_part",
    )(own, cols, lat, ogt, ogt)


def proj_kernel(after, ogt_ref, w_ref, out_ref, og):
    part = ogt_ref.shape[0] // 2

    @pl.when(pl.program_id(0) == 0)
    def _():
        for a in range(2):
            og[:, a * part : (a + 1) * part] = ogt_ref[a * part : (a + 1) * part, :].T

    out_ref[...] = mm(og[...], w_ref[...])


def proj_part(after, ogt, w):
    rows, tok = ogt.shape
    ff = w.shape[1]
    tile = 256
    return pl.pallas_call(
        proj_kernel,
        out_shape=jax.ShapeDtypeStruct((tok, ff), F32),
        grid_spec=pltpu.PrefetchScalarGridSpec(
            num_scalar_prefetch=1,
            grid=(ff // tile,),
            in_specs=[
                pl.BlockSpec((rows // 2, tok), lambda n, a: (0, 0)),
                pl.BlockSpec((rows // 2, tile), lambda n, a: (0, n)),
            ],
            out_specs=pl.BlockSpec((tok, tile), lambda n, a: (0, n)),
            scratch_shapes=[pltpu.VMEM((tok, rows // 2), BF)],
        ),
        compiler_params=params(16),
        cost_estimate=CHEAP,
        name="proj_part",
    )(after, ogt, w)


def back_kernel(after, cols_ref, ogt_ref, proj_ref, w_other, ct_ref, din_ref, h_ref, gh_ref, gg_ref, og, lhs):
    n = pl.program_id(0)
    cols = cols_ref[...]
    part = ogt_ref.shape[0] // 2
    rank = ct_ref.shape[2]

    @pl.when(n == 0)
    def _():
        for a in range(2):
            og[:, a * part : (a + 1) * part] = ogt_ref[a * part : (a + 1) * part, :].T
        for e in range(NZ):
            coef = ct_ref[e].astype(F32)
            for k in range(2):
                lhs[k, :, e * rank : (e + 1) * rank] = (column(cols, 8 + 8 * k + e) * coef).astype(BF)
        gg_ref[...] = jnp.zeros_like(gg_ref)

    proj = mm(og[...], w_other[...]) + proj_ref[...]
    for k in range(2):
        delta = mm_nt(lhs[k, :, :rank], din_ref[0])
        for e in range(1, NZ):
            delta = delta + mm_nt(lhs[k, :, e * rank : (e + 1) * rank], din_ref[e])
        back = proj + delta
        gh_ref[k] = (column(cols, 32 + k) * back).astype(BF)
        gg_ref[k] += jnp.sum(h_ref[k].astype(F32) * back, axis=1, keepdims=True)


def back_pass(after, cols, ogt, proj, w_other, ct, din, hk):
    tok, ff = hk.shape[1:]
    rows = ogt.shape[0]
    rank = din.shape[2]
    tile = 256
    w_spec = pl.BlockSpec((rows // 2, tile), lambda n, a: (0, n))
    return pl.pallas_call(
        back_kernel,
        out_shape=(
            jax.ShapeDtypeStruct((2, tok, ff), BF),
            jax.ShapeDtypeStruct((2, tok, 1), F32),
        ),
        grid_spec=pltpu.PrefetchScalarGridSpec(
            num_scalar_prefetch=1,
            grid=(ff // tile,),
            in_specs=[
                pl.BlockSpec((tok, 128), lambda n, a: (0, 0)),
                pl.BlockSpec((rows // 2, tok), lambda n, a: (1, 0)),
                pl.BlockSpec((tok, tile), lambda n, a: (0, n)),
                w_spec,
                pl.BlockSpec((NZ, tok, rank), lambda n, a: (0, 0, 0)),
                pl.BlockSpec((NZ, tile, rank), lambda n, a: (0, n, 0)),
                pl.BlockSpec((2, tok, tile), lambda n, a: (0, 0, n)),
            ],
            out_specs=[
                pl.BlockSpec((2, tok, tile), lambda n, a: (0, 0, n)),
                pl.BlockSpec((2, tok, 1), lambda n, a: (0, 0, 0)),
            ],
            scratch_shapes=[pltpu.VMEM((tok, rows // 2), BF), pltpu.VMEM((2, tok, NZ * rank), BF)],
        ),
        compiler_params=params(36),
        cost_estimate=CHEAP,
        name="back_pass",
    )(after, cols, ogt, proj, w_other, ct, din, hk)


def add(a, b):
    return (a.astype(F32) + b.astype(F32)).astype(BF)


def tie_kernel(*refs):
    del refs


def tie(arrays):
    return pl.pallas_call(
        tie_kernel,
        out_shape=tuple(jax.ShapeDtypeStruct(v.shape, v.dtype) for v in arrays),
        in_specs=[pl.BlockSpec(memory_space=pl.ANY)] * len(arrays),
        out_specs=tuple(pl.BlockSpec(memory_space=pl.ANY) for _ in arrays),
        input_output_aliases={i: i for i in range(len(arrays))},
        compiler_params=pltpu.CompilerParams(has_side_effects=False, vmem_limit_bytes=1024 * 1024),
        cost_estimate=CHEAP,
        name="tie",
    )(*arrays)


def exchange(sends, pins):
    arrays, places = [], []
    for v in [v for v, _, _ in sends] + list(pins):
        same = [i for i, w in enumerate(arrays) if w is v]
        places.append(same[0] if same else len(arrays))
        if not same:
            arrays.append(v)
    tied = tie(arrays)
    tied = [tied[i] for i in places]
    got = [lax.ppermute(v, axis, pairs) for v, (_, axis, pairs) in zip(tied, sends)]
    return got, tied[len(sends) :], tied[: len(sends)]


def core(v):
    return (v, "dp", CORE_PAIRS)


def wide(sends, t):
    return [(sends[s], "dp", step_pairs(s, t)) for s in range(2)]


LOW = ((0,), (1,), (0, 1))


def low(blocks):
    return [(v, "dp", step_pairs(0, *bits)) for v, bits in zip(blocks, LOW)]


def split(keep, got, n):
    stay = [add(k[:n], g[:n]) for k, g in zip(keep, got)]
    go = [add(k[n : 2 * n], g[n : 2 * n]) for k, g in zip(keep, got)]
    return stay, go


def split_low(keep, got):
    out = [
        jnp.stack([add(k[i : i + 1], g[i : i + 1]) for k, g in zip(keep, got)]) for i in range(4)
    ]
    return out[0], out[1:]


def last(keep, got):
    total = keep.astype(F32)
    for g in got:
        total = total + g.astype(F32)
    return total


def by_z(v, by):
    return (v, "expert", [(z, (z + by) % NZ) for z in range(NZ)])


def across_z(v, by):
    return (v, "expert", [(z, z ^ by) for z in range(NZ)])


def on_device(hidden, out_grad, gate_probs, expert_ids, base_down, delta_in, delta_out):
    tok, _, ff = hidden.shape
    width = out_grad.shape[1]
    rank = delta_in.shape[2]
    dp, own = lax.axis_index("dp"), lax.axis_index("expert")
    pos = lax.dynamic_index_in_dim(jnp.asarray(position_table()), dp, 0, keepdims=False)
    zpos = lax.dynamic_index_in_dim(jnp.asarray(z_table()), own, 0, keepdims=False)
    own = own.astype(jnp.int32).reshape(1)

    block = base_down.T.reshape(2, 1, 48, ff)
    got, (pos,), sent = exchange(low([block] * 3), [pos])
    held = merge_low([sent[0]] + got)
    rows, cols, coef_mine, ogt = front(pos, own, expert_ids.T, gate_probs.T, out_grad, delta_out)
    ogt = ogt.reshape(width, tok)
    hk = jnp.transpose(hidden, (1, 0, 2))
    hg = (gate_probs.T[:, :, None] * hk.astype(F32)).sum(axis=0).astype(BF)

    got, (own1, zpos), sent = exchange(wide(held, 2) + [across_z(coef_mine, 1)], [own, zpos])
    held = merge([sent[:2], got[:2]])
    pair = jnp.stack([sent[2], got[2]])
    lat = latents(zpos, rows, cols, hk, delta_in)

    up = jnp.concatenate([pair, lat[6:7]], axis=0)
    down = jnp.concatenate([pair, lat[7:8]], axis=0)
    got, (own2,), sent = exchange(wide(held, 3) + [by_z(up, 2), by_z(down, -2)], [own1])
    w_own = merge_all(sent[:2], got[:2])
    back, ahead = got[2][:2], got[3][:2]
    up = jnp.concatenate([back[:1], add(lat[4:5], got[2][2:]), lat[5:6]], axis=0)
    down = jnp.concatenate([ahead[1:], lat[2:3], add(lat[3:4], got[3][2:])], axis=0)
    send = base_part(own2, hg, ogt, 1)
    base_keep = base_part(own2, hg, ogt, 0)

    got, (own3, base_keep), sent = exchange(
        [core(w_own), core(send.reshape(2, 16, 48, ff)), by_z(up, 2), by_z(down, -2)],
        [own2, base_keep],
    )
    base_keep = base_keep.reshape(2, 16, 48, ff)
    w_other = got[0]
    proj = proj_part(own3, ogt, sent[0].reshape(width // 2, ff))
    coefs = jnp.concatenate([pair, back, ahead, got[2][:1], got[3][:1]], axis=0)
    lat_mine, lat_mate = [last(lat[i], [got[2][1 + i], got[3][1 + i]]).astype(BF) for i in range(2)]
    base_keep, base_go = split(base_keep, got[1], 8)

    got, (own4, coefs, proj), _ = exchange(
        wide(base_go, 3) + [across_z(lat_mate, 1)], [own3, coefs, proj]
    )
    latent_b = add(lat_mine, got[2])
    in_keep, in_send, ct = delta_in_part(pos, zpos, cols, coefs, hk)
    base_keep, base_go = split(base_keep, got, 4)
    in_keep = in_keep.reshape(2, 16, 32, ff)

    got, (own5, latent_b), _ = exchange(
        wide(base_go, 2) + [core(in_send.reshape(2, 16, 32, ff))], [own4, latent_b]
    )
    gh, gg = back_pass(
        own5, cols, ogt, proj, w_other.reshape(width // 2, ff), ct, delta_in, hk
    )
    out_keep, out_send = [
        v.reshape(2, 16, 48, rank) for v in delta_out_part(own5, cols, latent_b, ogt)
    ]
    base_keep, base_go = split_low(base_keep, got)
    in_keep, in_go = split(in_keep, got[2], 8)

    gg = gg.reshape(2, tok)
    got, _, sent = exchange(
        wide(in_go, 3) + [core(out_send), across_z(gg, 1)] + low(base_go), []
    )
    grad_hidden = jnp.transpose(gh, (1, 0, 2))
    grad_base = last(base_keep, got[4:]).reshape(96, ff).T
    in_keep, in_go = split(in_keep, got[:2], 4)
    gg = sent[3] + got[3]
    cut = [
        [add(out_keep[r, 4 * i : 4 * i + 4], got[2][r, 4 * i : 4 * i + 4]) for r in range(2)]
        for i in range(4)
    ]
    out_keep = jnp.stack(cut[0])
    out_go = [
        jnp.stack([cut[1][0], cut[2][1]]),
        jnp.stack([cut[2][0], cut[1][1]]),
        jnp.stack(cut[3]),
    ]

    got, _, sent = exchange(
        wide(in_go, 2)
        + [(v, "dp", step_pairs(0, *bits)) for v, bits in zip(out_go, ((2,), (3,), (2, 3)))]
        + [across_z(gg, 2)],
        [],
    )
    in_keep, in_go = split_low(in_keep, got)
    total = last(out_keep, got[2:5]).astype(BF)
    gg = sent[5] + got[5]

    got, _, sent = exchange(
        low(in_go) + low([total[:, i : i + 1] for i in (1, 2, 3)]) + [across_z(gg, 4)], []
    )
    grad_delta_in = jnp.transpose(last(in_keep, got[:3]).reshape(NZ, 8, ff), (0, 2, 1))
    grad_delta_out = last(total[:, :1], got[3:6]).reshape(96, rank).T[None]
    gg = sent[6] + got[6]
    return grad_hidden, gg.T, grad_base, grad_delta_in, grad_delta_out


def solution(mesh):
    in_specs = (
        P("dp", None, "expert"),
        P("dp", None),
        P("dp", None),
        P("dp", None),
        P("expert", "dp"),
        P(None, "expert", None),
        P("expert", None, None),
    )
    out_specs = (
        P("dp", None, "expert"),
        P("dp", None),
        P("expert", "dp"),
        P(None, "expert", "dp"),
        P("expert", None, "dp"),
    )
    return jax.shard_map(
        on_device, mesh=mesh, in_specs=in_specs, out_specs=out_specs, check_vma=False
    )
```
